256 devices in a mesh: tm: 32 (over y, z_hi, x), dp: 8 (over z_lo, core).
Axes of the slice: x: 4, y: 4, z: 8 (z_hi: 2, z_lo: 4; z = z_hi * 4 + z_lo), core: 2. Of those that a mesh axis runs over, the one named last changes fastest.
Arguments:
- queries: bfloat16 [8, 8192, 1664], P('dp', 'tm'), may hold values from -5 to 5
- keys: bfloat16 [8, 8192, 1664], P('dp', 'tm'), may hold values from -5 to 5
- values: bfloat16 [8, 8192, 1664], P('dp', 'tm'), may hold values from -6 to 6
- grad_out: bfloat16 [8, 8192, 3200], P('dp', 'tm'), may hold values from -1.5 to 1.5
- out_weight: bfloat16 [1664, 3200], P(None, 'dp'), may hold values from -0.15625 to 0.15625
- frame_clip: int32 [8, 32], P('dp'), may hold values from 0 to 4, never falling along the last dimension, each value on 1 to 12 neighbouring positions
Outputs:
- result: bfloat16 [8, 8192, 3200], P('dp', 'tm')
- grad_queries: bfloat16 [8, 8192, 1664], P('dp', 'tm')
- grad_keys: bfloat16 [8, 8192, 1664], P('dp', 'tm')
- grad_values: bfloat16 [8, 8192, 1664], P('dp', 'tm')
- grad_weight: bfloat16 [1664, 3200], P('tm', 'dp')
The draws below stay inside these ranges and needn't reach their ends.
All inputs are finite; a program needn't handle non-finite values.
Results may differ from the reference program's by a relative error of at most 0.025.
Values may be sent and summed in bfloat16 or wider, within the bound.
A program may use at most 192 MiB of HBM per device.

```python
import math
import jax
import jax.numpy as jnp
import numpy as np
from jax import lax

D = 3200
HEADS = 13
HS = 128
P_SIZE = 256
HD = 1664
FRAMES = 32
TOKENS = 8192
PACKS = 8
N_TM = 32


def draw_queries(key, part):
    key = jax.random.fold_in(key, 11)
    drawn = jnp.clip(jax.random.normal(key, (PACKS, TOKENS, HD), jnp.float32), -5.0, 5.0)
    return drawn.astype(jnp.bfloat16)


def draw_keys(key, part):
    key = jax.random.fold_in(key, 23)
    drawn = jnp.clip(jax.random.normal(key, (PACKS, TOKENS, HD), jnp.float32), -5.0, 5.0)
    return drawn.astype(jnp.bfloat16)


def with_spikes(values, rng, source, target, shards_of, factor):
    def block_of(axis_at):
        return (jnp.arange(values.shape[axis_at]) // (values.shape[axis_at] // shards_of)).reshape((-1,) + (1,) * (values.ndim - 1 - axis_at))

    near = jax.random.permutation(rng, shards_of)[block_of(target)]
    second = (block_of(target) + shards_of // 2) % shards_of
    return jnp.where((block_of(source) == near) | (block_of(source) == second), factor * values, values)


def shard_levels(stream_key, extent, cuts, low, top_value):
    def one(position, blocks):
        steps = jax.random.uniform(jax.random.fold_in(jax.random.fold_in(stream_key, 6), position), (blocks,), jnp.float32, low / len(cuts), top_value / len(cuts))
        return jnp.repeat(jnp.exp(steps), extent[position] // blocks).reshape((-1,) + (1,) * (len(extent) - position - 1))

    level = one(*cuts[0])
    for cut in cuts[1:]:
        level = level * one(*cut)
    return level


def split_up(number_of, total, most, slope):
    portions = [(1 << 20) // math.isqrt(grade ** slope) + 1 for grade in range(2, number_of + 1)]
    surplus, given = total - most - (number_of - 1), [1] * (number_of - 1)
    while surplus > 0:
        candidates = [i for i in range(number_of - 1) if given[i] < most]
        pool, left = sum([portions[i] for i in candidates]), surplus
        for i in candidates:
            more = min(most - given[i], max(1, left * portions[i] // pool), surplus)
            given[i] = given[i] + more
            surplus = surplus - more
    return np.array([most] + given)


def uneven_parts(stream_key, number_of, total, bound, skew):
    if number_of == 2:
        one = jax.random.randint(stream_key, (), max(1, total - bound), min(bound, total - 1) + 1)
        return jnp.stack([one, total - one])
    sizes = jnp.asarray(split_up(number_of, total, bound, skew), jnp.int32)
    twos = (number_of - 1) // 2
    giver, taker = sizes[1:1 + 2 * twos:2], sizes[2:2 + 2 * twos:2]
    room = jnp.minimum(giver - 1, bound - taker)
    shifted = jax.random.randint(jax.random.fold_in(stream_key, 1), (twos,), 0, 1 << 20) % (room + 1)
    sizes = sizes.at[1:1 + 2 * twos:2].set(giver - shifted).at[2:2 + 2 * twos:2].set(taker + shifted)
    return sizes[jax.random.permutation(jax.random.fold_in(stream_key, 2), number_of)]


def bell_draw(key, shape, deviation, most, pieces=(), kind=jnp.bfloat16):
    values = jax.random.normal(key, shape, jnp.float32) * deviation
    if len(pieces) > 0:
        values = shard_levels(key, shape, pieces, -0.22, 0.18) * values
    return jnp.clip(values, min=-most, max=most).astype(kind)


def heavy_noise(own_key, dims, spread, bound, pieces, heavy, held_as=jnp.bfloat16):
    values = spread * jax.random.normal(own_key, dims, jnp.float32)
    if pieces:
        values = values * shard_levels(own_key, dims, pieces, -0.22, 0.18)
    return jnp.clip(with_spikes(values, jax.random.fold_in(own_key, 3), *heavy), -bound, bound).astype(held_as)


def setup_inputs(seed: int = 0) -> dict:
    arg_keys = jax.random.split(jax.random.key(seed), 7)
    queries = draw_queries(jax.random.fold_in(arg_keys[6], 71), 0)
    keys = draw_keys(jax.random.fold_in(arg_keys[6], 71), 0)
    values = bell_draw(arg_keys[2], (PACKS, TOKENS, HD), 1.0, 6.0, ((0, 8), (1, 32)))
    grad_out = heavy_noise(arg_keys[3], (PACKS, TOKENS, D), 0.25, 1.5, ((0, 8), (1, 32)), (1, 2, 32, 2.75))
    out_weight = bell_draw(arg_keys[4], (HD, D), HD ** -0.5, 0.15625, ((1, 8),))
    frame_clip = jax.vmap(lambda own: jnp.searchsorted(jnp.cumsum(uneven_parts(own, FRAMES // 6, FRAMES, 12, 2)), jnp.arange(FRAMES), side="right"))(jax.random.split(arg_keys[5], PACKS)).reshape((PACKS, FRAMES)).astype(jnp.int32)
    return {"queries": queries, "keys": keys, "values": values, "grad_out": grad_out, "out_weight": out_weight, "frame_clip": frame_clip}


def key_windows(field):
    padded = jnp.pad(field, ((1, 1), (0, 0), (0, 0), (0, 0)))
    return jnp.concatenate([padded[:-2], padded[1:-1], padded[2:]], axis=1)

def spread_back(window):
    parts = [window[:, t * P_SIZE:(t + 1) * P_SIZE] for t in range(3)]
    total = jnp.pad(parts[0], ((0, 2), (0, 0), (0, 0), (0, 0)))
    total = total + jnp.pad(parts[1], ((1, 1), (0, 0), (0, 0), (0, 0)))
    total = total + jnp.pad(parts[2], ((2, 0), (0, 0), (0, 0), (0, 0)))
    return total[1:-1]

def frame_scores(query_frame, key_window, allowed):
    scores = jnp.einsum('qhd,khd->hqk', query_frame.astype(jnp.float32), key_window.astype(jnp.float32)) * HS ** (-0.5)
    live = jnp.repeat(allowed, P_SIZE)[None, None, :]
    return (scores, live)

def attend(query_frame, key_window, value_window, allowed):
    scores, live = frame_scores(query_frame, key_window, allowed)
    peak = lax.optimization_barrier(jnp.max(jnp.where(live, scores, -1e+30), axis=-1, keepdims=True))
    expo = jnp.where(live, jnp.exp(scores - peak), 0.0)
    total = lax.optimization_barrier(jnp.sum(expo, axis=-1, keepdims=True))
    weights = lax.optimization_barrier((expo / total).astype(jnp.bfloat16)).astype(jnp.float32)
    mixed = jnp.einsum('hqk,khd->qhd', weights, value_window.astype(jnp.float32)).astype(jnp.bfloat16)
    return (mixed, (peak + jnp.log(total))[..., 0])

def backprop(query_frame, key_window, value_window, allowed, grad_frame, lse, delta):
    scores, live = frame_scores(query_frame, key_window, allowed)
    probs = jnp.where(live, jnp.exp(scores - lse[..., None]), 0.0)
    rounded_probs = lax.optimization_barrier(probs.astype(jnp.bfloat16)).astype(jnp.float32)
    grad_frame32 = grad_frame.astype(jnp.float32)
    grad_vals = jnp.einsum('hqk,qhd->khd', rounded_probs, grad_frame32)
    grad_probs = jnp.einsum('qhd,khd->hqk', grad_frame32, value_window.astype(jnp.float32))
    grad_scores = probs * (grad_probs - delta[..., None])
    rounded = lax.optimization_barrier(grad_scores.astype(jnp.bfloat16)).astype(jnp.float32)
    grad_query = jnp.einsum('hqk,khd->qhd', rounded, key_window.astype(jnp.float32)) * HS ** (-0.5)
    grad_key = jnp.einsum('hqk,qhd->khd', rounded, query_frame.astype(jnp.float32)) * HS ** (-0.5)
    return (grad_query, grad_key, grad_vals)

def one_pack(pack):
    queries, keys, values, grad_out, out_weight, clip = pack
    shape4 = (FRAMES, P_SIZE, HEADS, HS)
    query_frames = queries.reshape(shape4)
    key_win = key_windows(keys.reshape(shape4))
    value_win = key_windows(values.reshape(shape4))
    extended = jnp.pad(clip, 1, constant_values=-1)
    allowed = jnp.stack([extended[:-2], extended[1:-1], extended[2:]], axis=1) == clip[:, None]
    mixed, lse = lax.map(lambda t: attend(*t), (query_frames, key_win, value_win, allowed))
    mixed_rows = mixed.reshape(TOKENS, HD)
    result = jnp.dot(mixed_rows, out_weight, preferred_element_type=jnp.float32).astype(jnp.bfloat16)
    grad_mixed = jnp.dot(grad_out, out_weight.T, preferred_element_type=jnp.float32).astype(jnp.bfloat16)
    grad_frames = grad_mixed.reshape(shape4)
    delta = jnp.einsum('fqhd,fqhd->fhq', grad_frames.astype(jnp.float32), mixed.astype(jnp.float32))
    grad_q, grad_kw, grad_vw = lax.map(lambda t: backprop(*t), (query_frames, key_win, value_win, allowed, grad_frames, lse, delta))
    grad_k = spread_back(grad_kw)
    grad_v = spread_back(grad_vw)
    return (result, grad_q.reshape(TOKENS, HD).astype(jnp.bfloat16), grad_k.reshape(TOKENS, HD).astype(jnp.bfloat16), grad_v.reshape(TOKENS, HD).astype(jnp.bfloat16), mixed_rows)

def weight_grad(mixed_all, grad_out):

    def pack_sum(total, pair):
        shards = pair[0].reshape(N_TM, -1, HD)
        grads = pair[1].reshape(N_TM, -1, D)

        def shard_sum(inner, piece):
            term = lax.dot_general(piece[0], piece[1], (((0,), (0,)), ((), ())), preferred_element_type=jnp.float32)
            return (inner + lax.optimization_barrier(term.astype(jnp.bfloat16)).astype(jnp.float32), None)
        inner, _ = lax.scan(shard_sum, jnp.zeros((HD, D), jnp.float32), (shards, grads))
        return (total + inner, None)
    total, _ = lax.scan(pack_sum, jnp.zeros((HD, D), jnp.float32), (mixed_all, grad_out))
    return total.astype(jnp.bfloat16)

def reference(queries, keys, values, grad_out, out_weight, frame_clip):
    weights_all = jnp.broadcast_to(out_weight, (PACKS, HD, D))
    result, grad_q, grad_k, grad_v, mixed_all = lax.map(one_pack, (queries, keys, values, grad_out, weights_all, frame_clip))
    return (result, grad_q, grad_k, grad_v, weight_grad(mixed_all, grad_out))
```

```python
import functools
import math

import jax
import jax.numpy as jnp
from jax import lax
from jax.experimental import pallas as pl
from jax.experimental.pallas import tpu as pltpu
from jax.sharding import PartitionSpec as P

HS = 128
ROWS = 256
HD = 1664
HEADS = 13
BLOCK = 400
PIECE = 96
REST = 16
GROUPS = ((0, 4), (4, 7), (7, 10), (10, 13))
MESH = pl.DeviceIdType.MESH
F32 = jnp.float32
BF16 = jnp.bfloat16
SCALE = HS ** (-0.5)
SCALE2 = SCALE * math.log2(math.e)


class Copies:
    def __init__(self, send, recv):
        self.send, self.recv, self.count = send, recv, 0
        self.started = []

    def start(self, src, dst, device):
        copy = pltpu.make_async_remote_copy(
            src_ref=src,
            dst_ref=dst,
            send_sem=self.send.at[self.count],
            recv_sem=self.recv.at[self.count],
            device_id=device,
            device_id_type=MESH,
        )
        self.count += 1
        copy.start()
        self.started.append(copy)
        return copy


def nt(a, b):
    return lax.dot_general(a, b, (((1,), (1,)), ((), ())), preferred_element_type=F32)


def tn(a, b):
    return lax.dot_general(a, b, (((0,), (0,)), ((), ())), preferred_element_type=F32)


def nn(a, b):
    return lax.dot_general(a, b, (((1,), (0,)), ((), ())), preferred_element_type=F32)


N_COPIES = 79


def body(
    q, k, v, go, wt, bias,
    res, dq, dk, dv, gw,
    kw, vw, w, probs, mx, gm, gop, dsend, drecv, down, term, yr1, yr2, ysum, xs, xr, zs, zr,
    local, send, recv,
):
    tm = lax.axis_index("tm")
    dp = lax.axis_index("dp")
    x, zh, y = tm % 4, (tm // 4) % 2, tm // 8
    zl, c = dp // 2, dp % 2
    z = zh * 4 + zl

    def place(x_, y_, z_, c_):
        return ((y_ * 2 + z_ // 4) * 4 + x_, (z_ % 4) * 2 + c_)

    up = (lax.rem(tm + 1, 32), dp)
    down_dev = (lax.rem(tm + 31, 32), dp)
    peer = place(x, y, z, 1 - c)
    along_x = [place(lax.rem(x + d, 4), y, z, c) for d in (1, 2, 3)]
    along_y = [place(x, lax.rem(y + d, 4), z, c) for d in (1, 2, 3)]
    along_z = [place(x, y, lax.rem(z + d, 8), c) for d in range(1, 8)]
    partners = [up, down_dev, peer] + along_x + along_y + along_z

    barrier = pltpu.get_barrier_semaphore()
    for device in partners:
        pl.semaphore_signal(barrier, inc=1, device_id=device, device_id_type=MESH)

    own_k = pltpu.make_async_copy(k, kw.at[pl.ds(ROWS, ROWS)], local.at[0])
    own_v = pltpu.make_async_copy(v, vw.at[pl.ds(ROWS, ROWS)], local.at[1])
    own_block = pl.multiple_of(zl * BLOCK, 16)
    own_w = pltpu.make_async_copy(wt, w.at[c, pl.ds(own_block, BLOCK)], local.at[2])
    own_k.start()
    own_v.start()
    own_w.start()
    for i in range(2):
        w[i, pl.ds(4 * BLOCK, HD - 4 * BLOCK), :] = jnp.zeros((HD - 4 * BLOCK, HD), BF16)

    copies = Copies(send, recv)
    pl.semaphore_wait(barrier, len(partners))

    def piece_at(block, at):
        return pl.ds(pl.multiple_of(block * BLOCK + at * PIECE, 16), PIECE)

    def rest_at(block):
        return pl.ds(pl.multiple_of(block * BLOCK + 4 * PIECE, 16), REST)

    w_z = []
    second = place(x, y, lax.rem(z + 2 + 4 * c, 8), c)
    for device in (along_z[0], along_z[6], second):
        w_z.append(copies.start(
            wt.at[pl.ds(pl.multiple_of(y * PIECE, 16), PIECE)], w.at[c, piece_at(zl, y)], device))
        w_z.append(copies.start(wt.at[pl.ds(4 * PIECE, REST)], w.at[c, rest_at(zl)], device))

    halo = []
    for first, last in GROUPS:
        lanes = pl.ds(first * HS, (last - first) * HS)
        group = []
        for src, dst in ((k, kw), (v, vw)):
            group.append(copies.start(src.at[:, lanes], dst.at[pl.ds(0, ROWS), lanes], up))
            group.append(copies.start(src.at[:, lanes], dst.at[pl.ds(2 * ROWS, ROWS), lanes], down_dev))
        halo.append(group)
    w_peer = [copies.start(wt, w.at[c, pl.ds(own_block, BLOCK)], peer)]
    go_peer = copies.start(go.at[1 - c], gop, peer)

    others = [lax.rem(zl + d, 4) for d in (1, 2, 3)]
    for copy in w_z:
        copy.wait_recv()
    w_y = []
    for device in along_y:
        for block in others:
            at = piece_at(block, y)
            w_y.append(copies.start(w.at[c, at], w.at[c, at], device))
    for block in others:
        for at in (piece_at(block, y), rest_at(block)):
            w_peer.append(copies.start(w.at[c, at], w.at[c, at], peer))

    own_k.wait()
    own_v.wait()
    own_w.wait()

    def forward(h, carry):
        lanes = pl.ds(pl.multiple_of(h * HS, HS), HS)
        s = nt(q[:, lanes], kw[:, lanes]) * SCALE2 + bias[...]
        e = jnp.exp2(s - jnp.max(s, axis=-1, keepdims=True))
        p = (e * (1.0 / jnp.sum(e, axis=-1, keepdims=True))).astype(BF16)
        probs[h] = p
        mx[0, :, lanes] = nn(p, vw[:, lanes]).astype(BF16)
        return carry

    def w_along_y():
        for i, d in enumerate((1, 2, 3)):
            for j, block in enumerate(others):
                w_y[3 * i + j].wait_recv()
                at = piece_at(block, lax.rem(y + 4 - d, 4))
                w_peer.append(copies.start(w.at[c, at], w.at[c, at], peer))

    for index, (first, last) in enumerate(GROUPS):
        if index == 3:
            w_along_y()
        for copy in halo[index]:
            copy.wait_recv()
        lax.fori_loop(first, last, forward, 0)
    mx_peer = copies.start(mx.at[0], mx.at[1], peer)

    for copy in w_peer:
        copy.wait_recv()

    def backward(h, carry):
        lanes = pl.ds(pl.multiple_of(h * HS, HS), HS)
        g = gm[:, lanes]
        p = probs[h]
        delta = jnp.sum(g.astype(F32) * mx[0, :, lanes].astype(F32), axis=-1, keepdims=True)
        ds = (p.astype(F32) * (nt(g, vw[:, lanes]) - delta)).astype(BF16)
        dq[:, lanes] = (nn(ds, kw[:, lanes]) * SCALE).astype(BF16)
        for which, grad in ((0, tn(ds, q[:, lanes]) * SCALE), (1, tn(p, g))):
            dsend[0, which, :, lanes] = grad[:ROWS].astype(BF16)
            down[which, :, lanes] = grad[ROWS : 2 * ROWS]
            dsend[1, which, :, lanes] = grad[2 * ROWS :].astype(BF16)
        return carry

    grads = []
    for first, last in GROUPS:
        lanes = pl.ds(first * HS, (last - first) * HS)
        gm[:, lanes] = (nn(go[0], w[0, :, lanes]) + nn(go[1], w[1, :, lanes])).astype(BF16)
        lax.fori_loop(first, last, backward, 0)
        group = []
        for which in (0, 1):
            group.append(copies.start(dsend.at[0, which, :, lanes], drecv.at[0, which, :, lanes], down_dev))
            group.append(copies.start(dsend.at[1, which, :, lanes], drecv.at[1, which, :, lanes], up))
        grads.append(group)

    go_peer.wait_recv()
    mx_peer.wait_recv()

    def weight_term(h, carry):
        lanes = pl.ds(pl.multiple_of(h * HS, HS), HS)
        term[lanes, :] = (tn(mx[0, :, lanes], go[c]) + tn(mx[1, :, lanes], gop[...])).astype(BF16)
        return carry

    lax.fori_loop(0, HEADS, weight_term, 0)

    def chunk(at, half=None):
        if half is None:
            return pl.ds(pl.multiple_of(at * 416, 16), 416)
        return pl.ds(pl.multiple_of(at * 416 + half * 208, 16), 208)

    after, across, before = [lax.rem(y + d, 4) for d in (1, 2, 3)]
    y_first = [
        copies.start(term.at[chunk(across, 0)], yr1.at[0], along_y[0]),
        copies.start(term.at[chunk(across, 1)], yr1.at[1], along_y[2]),
    ]

    def project(i):
        for at, size in ((0, 640), (640, 512), (1152, 512)):
            res[i, :, at : at + size] = nt(mx[0], w[i, at : at + size, :]).astype(BF16)

    project(0)
    y_second = []
    for half, target, device in ((0, after, along_y[0]), (1, before, along_y[2])):
        y_first[half].wait_recv()
        term[chunk(target, half), :] = (
            term[chunk(target, half), :].astype(F32) + yr1[half].astype(F32)
        ).astype(BF16)
        y_second.append(copies.start(term.at[chunk(target)], yr2.at[half], device))
    project(1)
    for copy in y_second:
        copy.wait_recv()
    ysum[pl.ds(416, 16), :] = jnp.zeros((16, HD), F32)
    ysum[pl.ds(0, 416), :] = (
        term[chunk(y), :].astype(F32) + yr2[0].astype(F32) + yr2[1].astype(F32)
    )
    for to in range(4):
        for half in range(2):
            xs[to, half] = ysum[pl.ds(208 * half + 52 * to, 64), :].astype(BF16)
    x_copies = [
        copies.start(xs.at[lax.rem(x + d, 4)], xr.at[d - 1], along_x[d - 1]) for d in (1, 2, 3)
    ]
    for copy in x_copies:
        copy.wait_recv()
    for half in range(2):
        total = xs[x, half].astype(F32)
        for i in range(3):
            total = total + xr[i, half].astype(F32)
        for block in range(4):
            turned = total if block == 0 else pltpu.roll(total, HD - BLOCK * block, 1)
            zs[half * 4 + block] = turned[:, :512].astype(BF16)
    z_copies = [
        copies.start(zs.at[lax.rem(z + d, 8)], zr.at[d - 1], along_z[d - 1]) for d in range(1, 8)
    ]
    for copy in z_copies:
        copy.wait_recv()
    total = zs[z].astype(F32)
    for i in range(7):
        total = total + zr[i].astype(F32)
    gw[...] = total.astype(BF16)

    for (first, last), group in zip(GROUPS, grads):
        lanes = pl.ds(first * HS, (last - first) * HS)
        for copy in group:
            copy.wait_recv()
        for which, out in ((0, dk), (1, dv)):
            out[:, lanes] = (
                down[which, :, lanes]
                + drecv[0, which, :, lanes].astype(F32)
                + drecv[1, which, :, lanes].astype(F32)
            ).astype(BF16)
    for copy in copies.started:
        copy.wait_send()


def on_device(queries, keys, values, grad_out, out_weight, frame_clip):
    tm = lax.axis_index("tm")
    extended = jnp.pad(frame_clip[0], 1, constant_values=-1)
    near = lax.dynamic_slice_in_dim(extended, tm, 3)
    bias = jnp.repeat(jnp.where(near == near[1], 0.0, -1e30).astype(F32), ROWS)[None]
    go = grad_out[0].reshape(ROWS, 4, 2, BLOCK).transpose(2, 0, 1, 3).reshape(2, ROWS, 4 * BLOCK)
    go = jnp.pad(go, ((0, 0), (0, 0), (0, HD - 4 * BLOCK)))
    vmem = pl.BlockSpec(memory_space=pltpu.VMEM)
    hbm = pl.BlockSpec(memory_space=pl.ANY)
    half = jax.ShapeDtypeStruct((ROWS, HD), BF16)
    res, dq, dk, dv, gw = pl.pallas_call(
        body,
        out_shape=(
            jax.ShapeDtypeStruct((2, ROWS, HD), BF16),
            half,
            half,
            half,
            jax.ShapeDtypeStruct((64, 512), BF16),
        ),
        in_specs=[vmem, hbm, hbm, vmem, vmem, vmem],
        out_specs=(vmem,) * 5,
        scratch_shapes=[
            pltpu.VMEM((3 * ROWS, HD), BF16),
            pltpu.VMEM((3 * ROWS, HD), BF16),
            pltpu.VMEM((2, HD, HD), BF16),
            pltpu.VMEM((HEADS, ROWS, 3 * ROWS), BF16),
            pltpu.VMEM((2, ROWS, HD), BF16),
            pltpu.VMEM((ROWS, HD), BF16),
            pltpu.VMEM((ROWS, HD), BF16),
            pltpu.VMEM((2, 2, ROWS, HD), BF16),
            pltpu.VMEM((2, 2, ROWS, HD), BF16),
            pltpu.VMEM((2, ROWS, HD), F32),
            pltpu.VMEM((HD, HD), BF16),
            pltpu.VMEM((2, 208, HD), BF16),
            pltpu.VMEM((2, 416, HD), BF16),
            pltpu.VMEM((432, HD), F32),
            pltpu.VMEM((4, 2, 64, HD), BF16),
            pltpu.VMEM((3, 2, 64, HD), BF16),
            pltpu.VMEM((8, 64, 512), BF16),
            pltpu.VMEM((7, 64, 512), BF16),
            pltpu.SemaphoreType.DMA((3,)),
            pltpu.SemaphoreType.DMA((N_COPIES,)),
            pltpu.SemaphoreType.DMA((N_COPIES,)),
        ],
        compiler_params=pltpu.CompilerParams(
            collective_id=0, has_side_effects=True, vmem_limit_bytes=63 * 1024 * 1024
        ),
        cost_estimate=pl.CostEstimate(flops=12_100_000_000, bytes_accessed=25_000_000, transcendentals=2_600_000),
        name="attention_and_projection",
    )(queries[0], keys[0], values[0], go, out_weight.T, bias)
    result = res[:, :, : 4 * BLOCK].reshape(2, ROWS, 4, BLOCK).transpose(1, 2, 0, 3)
    return (
        result.reshape(1, ROWS, 8 * BLOCK),
        dq[None],
        dk[None],
        dv[None],
        gw[:52, :BLOCK],
    )


def solution(mesh):
    in_specs = (
        P("dp", "tm", None),
        P("dp", "tm", None),
        P("dp", "tm", None),
        P("dp", "tm", None),
        P(None, "dp"),
        P("dp", None),
    )
    out_specs = (
        P("dp", "tm", None),
        P("dp", "tm", None),
        P("dp", "tm", None),
        P("dp", "tm", None),
        P("tm", "dp"),
    )
    return jax.shard_map(
        on_device, mesh=mesh, in_specs=in_specs, out_specs=out_specs, check_vma=False
    )
```

```python
import functools
import math

import jax
import jax.numpy as jnp
from jax import lax
from jax.experimental import pallas as pl
from jax.experimental.pallas import tpu as pltpu
from jax.sharding import PartitionSpec as P

HS = 128
ROWS = 256
HD = 1664
HEADS = 13
BLOCK = 400
PIECE = 96
REST = 16
GROUPS = ((0, 3), (3, 6), (6, 9), (9, 11), (11, 13))
ORDER = (3, 4, 0, 1, 2)
HALF = 896
WIDE = 1664
MESH = pl.DeviceIdType.MESH
F32 = jnp.float32
BF16 = jnp.bfloat16
SCALE = HS ** (-0.5)
SCALE2 = SCALE * math.log2(math.e)


class Copies:
    def __init__(self, send, recv):
        self.send, self.recv, self.count = send, recv, 0
        self.started = []

    def start(self, src, dst, device):
        copy = pltpu.make_async_remote_copy(
            src_ref=src,
            dst_ref=dst,
            send_sem=self.send.at[self.count],
            recv_sem=self.recv.at[self.count],
            device_id=device,
            device_id_type=MESH,
        )
        self.count += 1
        copy.start()
        self.started.append(copy)
        return copy


def nt(a, b):
    return lax.dot_general(a, b, (((1,), (1,)), ((), ())), preferred_element_type=F32)


def tn(a, b):
    return lax.dot_general(a, b, (((0,), (0,)), ((), ())), preferred_element_type=F32)


def nn(a, b):
    return lax.dot_general(a, b, (((1,), (0,)), ((), ())), preferred_element_type=F32)


N_COPIES = 47


class Beside:
    def __init__(self, x, up, down, mid_up, mid_down, over_up, over_down, to_up, to_down, held, sems):
        self.x, self.up, self.down = x, up, down
        self.mid_up, self.mid_down = mid_up, mid_down
        self.over_up, self.over_down = over_up, over_down
        self.to_up, self.to_down, self.held = to_up, to_down, held
        self.send, self.recv, self.in_send, self.in_recv, self.on_send = sems

    def direct(self, group, which, way):
        first, last = GROUPS[group]
        lanes = pl.ds(first * HS, (last - first) * HS)
        src, dst = (self.to_up, self.to_down)[way](which, lanes)
        at = (group * 2 + which) * 2 + way
        return pltpu.make_async_remote_copy(
            src_ref=src, dst_ref=dst, send_sem=self.send.at[at], recv_sem=self.recv.at[at],
            device_id=(self.up, self.down)[way], device_id_type=MESH,
        )

    def into(self, group, which, way):
        first, last = GROUPS[group]
        lanes = pl.ds(first * HS, (last - first) * HS)
        src, _ = (self.to_up, self.to_down)[way](which, lanes)
        at = way * 2 + which
        return pltpu.make_async_remote_copy(
            src_ref=src, dst_ref=self.held.at[way, which], send_sem=self.in_send.at[at], recv_sem=self.in_recv.at[at],
            device_id=(self.mid_up, self.mid_down)[way][group - 3], device_id_type=MESH,
        )

    def onward(self, group, which, way):
        first, last = GROUPS[group]
        lanes = pl.ds(first * HS, (last - first) * HS)
        _, dst = (self.to_up, self.to_down)[way](which, lanes)
        return pltpu.make_async_remote_copy(
            src_ref=self.held.at[way, which], dst_ref=dst, send_sem=self.on_send.at[way * 2 + which],
            recv_sem=self.recv.at[(group * 2 + which) * 2 + way],
            device_id=(self.over_up, self.over_down)[way], device_id_type=MESH,
        )

    def inner(self, way):
        return self.x != (3, 0)[way]

    def start_inner(self, groups):
        for way in (0, 1):
            @pl.when(self.inner(way))
            def _():
                for group in groups:
                    for which in (0, 1):
                        self.direct(group, which, way).start()

    def start_into(self, group):
        for way in (0, 1):
            @pl.when(jnp.logical_not(self.inner(way)))
            def _():
                for which in (0, 1):
                    self.into(group, which, way).start()

    def start_over(self, groups):
        for way in (0, 1):
            @pl.when(jnp.logical_not(self.inner(way)))
            def _():
                for group in groups:
                    for which in (0, 1):
                        self.direct(group, which, way).start()

    def pass_on(self):
        for column in (1, 2):
            @pl.when(self.x == column)
            def _():
                for way in (0, 1):
                    group = 3 if (way == 0) == (column == 2) else 4
                    for which in (0, 1):
                        self.into(group, which, way).wait_recv()
                        self.onward(group, which, way).start()

    def wait(self, group):
        for way in (0, 1):
            for which in (0, 1):
                self.direct(group, which, way).wait_recv()

    def drain(self):
        for way in (0, 1):
            for which in (0, 1):
                for group in range(3):
                    self.direct(group, which, way).wait_send()

                @pl.when(self.inner(way))
                def _():
                    for group in (3, 4):
                        self.direct(group, which, way).wait_send()

                @pl.when(jnp.logical_not(self.inner(way)))
                def _():
                    for group in (3, 4):
                        self.into(group, which, way).wait_send()

                @pl.when(jnp.logical_or(self.x == 1, self.x == 2))
                def _():
                    self.onward(3, which, way).wait_send()


def body(
    q, k, v, go, weight, clip,
    res, dq, dk, dv, gw,
    kw, vw, w, bias, probs, mx, gm, gop, dsend, drecv, down, held_kv, held_grad,
    term, yr1, yr2, ysum, xs, xr, zs, zr,
    local, send, recv, z_send, z_recv, *edge_sems,
):
    tm = lax.axis_index("tm")
    dp = lax.axis_index("dp")
    x, zh, y = tm % 4, (tm // 4) % 2, tm // 8
    zl, c = dp // 2, dp % 2
    z = zh * 4 + zl

    def place(x_, y_, z_, c_):
        return ((y_ * 2 + z_ // 4) * 4 + x_, (z_ % 4) * 2 + c_)

    def in_row(x_, step):
        return (lax.rem(tm // 4 + 8 + step, 8) * 4 + x_, dp)

    up = (lax.rem(tm + 1, 32), dp)
    down_dev = (lax.rem(tm + 31, 32), dp)
    peer = place(x, y, z, 1 - c)
    along_x = [place(lax.rem(x + d, 4), y, z, c) for d in (1, 2, 3)]
    along_y = [place(x, lax.rem(y + d, 4), z, c) for d in (1, 2, 3)]
    along_z = [place(x, y, lax.rem(z + d, 8), c) for d in range(1, 8)]
    across_z = [place(x, y, lax.rem(z + d, 8), 1 - c) for d in range(1, 8)]
    partners = [up, down_dev, peer] + along_x + along_y + along_z + across_z

    barrier = pltpu.get_barrier_semaphore()
    for device in partners:
        pl.semaphore_signal(barrier, inc=1, device_id=device, device_id_type=MESH)
    for column, step in ((0, -1), (3, 1)):
        @pl.when(x == column)
        def _():
            for column_ in (1, 2):
                pl.semaphore_signal(barrier, inc=1, device_id=in_row(column_, step), device_id_type=MESH)

    own_k = pltpu.make_async_copy(k, kw.at[pl.ds(ROWS, ROWS)], local.at[0])
    own_v = pltpu.make_async_copy(v, vw.at[pl.ds(ROWS, ROWS)], local.at[1])
    own_k.start()
    own_v.start()
    own = pl.ds(pl.multiple_of(dp * BLOCK, 16), BLOCK)
    for h in range(HEADS):
        w[own, h * HS : (h + 1) * HS] = weight[h * HS : (h + 1) * HS, :].T
    here = clip[0, tm]
    before_off = jnp.where(jnp.logical_and(tm > 0, clip[0, lax.rem(tm + 31, 32)] == here), 0.0, -1e30).astype(F32)
    after_off = jnp.where(jnp.logical_and(tm < 31, clip[0, lax.rem(tm + 1, 32)] == here), 0.0, -1e30).astype(F32)
    bias[:, pl.ds(0, ROWS)] = jnp.full((8, ROWS), before_off, F32)
    bias[:, pl.ds(ROWS, ROWS)] = jnp.zeros((8, ROWS), F32)
    bias[:, pl.ds(2 * ROWS, ROWS)] = jnp.full((8, ROWS), after_off, F32)

    copies = Copies(send, recv)
    mid = ((in_row(2, 0), in_row(1, 0)), (in_row(1, 0), in_row(2, 0)))
    over = (in_row(0, 1), in_row(3, -1))
    windows = (kw, vw)
    inputs = (k, v)
    keys_values = Beside(
        x, up, down_dev, *mid, *over,
        lambda which, lanes: (inputs[which].at[:, lanes], windows[which].at[pl.ds(0, ROWS), lanes]),
        lambda which, lanes: (inputs[which].at[:, lanes], windows[which].at[pl.ds(2 * ROWS, ROWS), lanes]),
        held_kv, edge_sems[:5],
    )
    grads = Beside(
        x, up, down_dev, *mid, *over,
        lambda which, lanes: (dsend.at[1, which, :, lanes], drecv.at[1, which, :, lanes]),
        lambda which, lanes: (dsend.at[0, which, :, lanes], drecv.at[0, which, :, lanes]),
        held_grad, edge_sems[5:],
    )
    pl.semaphore_wait(barrier, len(partners) + 2 * jnp.logical_or(x == 1, x == 2).astype(jnp.int32))

    def piece_at(block, at):
        return w.at[pl.ds(pl.multiple_of(block * BLOCK + at * PIECE, 16), PIECE)]

    def rest_at(block):
        return w.at[pl.ds(pl.multiple_of(block * BLOCK + 4 * PIECE, 16), REST)]

    def same(ref, device):
        return copies.start(ref, ref, device)

    w_z = []
    second = place(x, y, lax.rem(z + 2 + 4 * c, 8), c)
    for device in (along_z[0], along_z[6], second):
        w_z.append(same(piece_at(dp, y), device))
        w_z.append(same(rest_at(dp), device))
    for group in (3, 4):
        keys_values.start_into(group)
    keys_values.start_inner(ORDER)
    w_peer = [same(w.at[own], peer)]
    go_peer = copies.start(go.at[:, pl.ds(pl.multiple_of(1536 * (1 - c), 128), WIDE)], gop, peer)

    others = [lax.rem(zl + d, 4) * 2 + c for d in (1, 2, 3)]
    for copy in w_z:
        copy.wait_recv()
    w_y = []
    for device in along_y:
        for block in others:
            w_y.append(same(piece_at(block, y), device))
    keys_values.start_over((0, 1, 2))
    for block in others:
        w_peer.append(same(piece_at(block, y), peer))
        w_peer.append(same(rest_at(block), peer))
    keys_values.pass_on()

    own_k.wait()
    own_v.wait()

    def forward(h, carry):
        lanes = pl.ds(pl.multiple_of(h * HS, HS), HS)
        s = nt(q[:, lanes], kw[:, lanes]) * SCALE2 + bias[0:1, :]
        e = jnp.exp2(s - jnp.max(s, axis=-1, keepdims=True))
        p = (e * (1.0 / jnp.sum(e, axis=-1, keepdims=True))).astype(BF16)
        probs[h] = p
        mx[0, :, lanes] = nn(p, vw[:, lanes]).astype(BF16)
        return carry

    def w_along_y():
        for i, d in enumerate((1, 2, 3)):
            for j, block in enumerate(others):
                w_y[3 * i + j].wait_recv()
                w_peer.append(same(piece_at(block, lax.rem(y + 4 - d, 4)), peer))

    for index, group in enumerate(ORDER):
        if index == 4:
            w_along_y()
        keys_values.wait(group)
        lax.fori_loop(*GROUPS[group], forward, 0)
    mx_peer = copies.start(mx.at[0], mx.at[1], peer)

    go_peer.wait_recv()
    mx_peer.wait_recv()

    def chunk(p, at, half=None):
        if half is None:
            return term.at[p, pl.ds(pl.multiple_of(at * 416, 16), 416)]
        return term.at[p, pl.ds(pl.multiple_of(at * 416 + half * 208, 16), 208)]

    after, across, before = [lax.rem(y + d, 4) for d in (1, 2, 3)]
    y_first, y_second, x_copies = [], [], []
    for p in (0, 1):
        def weight_term(h, carry):
            lanes = pl.ds(pl.multiple_of(h * HS, HS), HS)
            columns = pl.ds(pl.multiple_of(1536 * c + 768 * p, 128), HALF)
            term[p, lanes, :] = (
                tn(mx[0, :, lanes], go[:, columns]) + tn(mx[1, :, lanes], gop[:, 768 * p : 768 * p + HALF])
            ).astype(BF16)
            return carry

        lax.fori_loop(0, HEADS, weight_term, 0)
        y_first.append([
            copies.start(chunk(p, across, 0), yr1.at[p, 0], along_y[0]),
            copies.start(chunk(p, across, 1), yr1.at[p, 1], along_y[2]),
        ])

    def y_next(p):
        pair = []
        for half, target, device in ((0, after, along_y[0]), (1, before, along_y[2])):
            y_first[p][half].wait_recv()
            part = chunk(p, target, half)
            part[...] = (part[...].astype(F32) + yr1[p, half].astype(F32)).astype(BF16)
            pair.append(copies.start(chunk(p, target), yr2.at[p, half], device))
        y_second.append(pair)

    for copy in w_peer:
        copy.wait_recv()

    def backward(h, carry):
        lanes = pl.ds(pl.multiple_of(h * HS, HS), HS)
        g = gm[:, lanes]
        p = probs[h]
        delta = jnp.sum(g.astype(F32) * mx[0, :, lanes].astype(F32), axis=-1, keepdims=True)
        ds = (p.astype(F32) * (nt(g, vw[:, lanes]) - delta)).astype(BF16)
        dq[:, lanes] = (nn(ds, kw[:, lanes]) * SCALE).astype(BF16)
        for which, grad in ((0, tn(ds, q[:, lanes]) * SCALE), (1, tn(p, g))):
            dsend[0, which, :, lanes] = grad[:ROWS].astype(BF16)
            down[which, :, lanes] = grad[ROWS : 2 * ROWS]
            dsend[1, which, :, lanes] = grad[2 * ROWS :].astype(BF16)
        return carry

    for index, group in enumerate(ORDER):
        first, last = GROUPS[group]
        lanes = pl.ds(first * HS, (last - first) * HS)
        gm[:, lanes] = nn(go[...], w[:, lanes]).astype(BF16)
        lax.fori_loop(first, last, backward, 0)
        if group > 2:
            grads.start_into(group)
        else:
            grads.start_over((group,))
        grads.start_inner((group,))
        if index in (1, 3):
            y_next(index // 2)

    for i in range(5):
        columns = pl.ds(i * 640, 640)
        res[:, columns] = nt(mx[0], w[columns, :]).astype(BF16)
    grads.pass_on()

    for p in (0, 1):
        for copy in y_second[p]:
            copy.wait_recv()
        ysum[pl.ds(0, 416), :] = (
            chunk(p, y)[...].astype(F32) + yr2[p, 0].astype(F32) + yr2[p, 1].astype(F32)
        )
        ysum[pl.ds(416, 16), :] = jnp.zeros((16, HALF), F32)
        for to in range(4):
            for half in range(2):
                xs[p, to, half] = ysum[pl.ds(208 * half + 52 * to, 64), :].astype(BF16)
        x_copies.append([
            copies.start(xs.at[p, lax.rem(x + d, 4)], xr.at[p, d - 1], along_x[d - 1]) for d in (1, 2, 3)
        ])

    def to_owner(p, half, b):
        at = p * 4 + half * 2 + b
        z_to = half * 4 + c * 2 + p
        slot = lax.rem(z + 8 - z_to, 8)
        mine = jnp.logical_and(z_to == z, c == b)
        return mine, at, pltpu.make_async_remote_copy(
            src_ref=zs.at[at], dst_ref=zr.at[slot], send_sem=z_send.at[at], recv_sem=z_recv.at[slot],
            device_id=place(x, y, z_to, b), device_id_type=MESH,
        )

    for p in (0, 1):
        for copy in x_copies[p]:
            copy.wait_recv()
        for half in range(2):
            total = xs[p, x, half].astype(F32)
            for i in range(3):
                total = total + xr[p, i, half].astype(F32)
            for b in (0, 1):
                shift = lax.rem(2 * HALF - BLOCK * b - 32 * p - 64 * c, HALF)
                zs[p * 4 + half * 2 + b] = pltpu.roll(total, shift, 1)[:, :512].astype(BF16)
        for half in range(2):
            for b in (0, 1):
                mine, at, copy = to_owner(p, half, b)

                @pl.when(mine)
                def _():
                    zr[0] = zs[at]

                @pl.when(jnp.logical_not(mine))
                def _():
                    copy.start()

    def from_z(slot):
        return pltpu.make_async_remote_copy(
            src_ref=zs.at[0], dst_ref=zr.at[slot], send_sem=z_send.at[0], recv_sem=z_recv.at[slot],
            device_id=peer, device_id_type=MESH,
        )

    for slot in range(1, 8):
        from_z(slot).wait_recv()

    @pl.when(zl // 2 != c)
    def _():
        from_z(0).wait_recv()

    total = zr[0].astype(F32)
    for i in range(1, 8):
        total = total + zr[i].astype(F32)
    gw[...] = total.astype(BF16)

    for group in ORDER:
        first, last = GROUPS[group]
        lanes = pl.ds(first * HS, (last - first) * HS)
        grads.wait(group)
        for which, out in ((0, dk), (1, dv)):
            out[:, lanes] = (
                down[which, :, lanes]
                + drecv[0, which, :, lanes].astype(F32)
                + drecv[1, which, :, lanes].astype(F32)
            ).astype(BF16)
    for copy in copies.started:
        copy.wait_send()
    keys_values.drain()
    grads.drain()
    for p in (0, 1):
        for half in range(2):
            for b in (0, 1):
                mine, at, copy = to_owner(p, half, b)

                @pl.when(jnp.logical_not(mine))
                def _():
                    copy.wait_send()


def on_device(queries, keys, values, grad_out, out_weight, frame_clip):
    vmem = pl.BlockSpec(memory_space=pltpu.VMEM)
    hbm = pl.BlockSpec(memory_space=pl.ANY)
    half = jax.ShapeDtypeStruct((ROWS, HD), BF16)
    edge = [pltpu.SemaphoreType.DMA((n,)) for n in (20, 20, 4, 4, 4)]
    res, dq, dk, dv, gw = pl.pallas_call(
        body,
        out_shape=(
            jax.ShapeDtypeStruct((ROWS, 8 * BLOCK), BF16),
            half,
            half,
            half,
            jax.ShapeDtypeStruct((64, 512), BF16),
        ),
        in_specs=[vmem, hbm, hbm, vmem, vmem, pl.BlockSpec(memory_space=pltpu.SMEM)],
        out_specs=(vmem,) * 5,
        scratch_shapes=[
            pltpu.VMEM((3 * ROWS, HD), BF16),
            pltpu.VMEM((3 * ROWS, HD), BF16),
            pltpu.VMEM((8 * BLOCK, HD), BF16),
            pltpu.VMEM((8, 3 * ROWS), F32),
            pltpu.VMEM((HEADS, ROWS, 3 * ROWS), BF16),
            pltpu.VMEM((2, ROWS, HD), BF16),
            pltpu.VMEM((ROWS, HD), BF16),
            pltpu.VMEM((ROWS, WIDE), BF16),
            pltpu.VMEM((2, 2, ROWS, HD), BF16),
            pltpu.VMEM((2, 2, ROWS, HD), BF16),
            pltpu.VMEM((2, ROWS, HD), F32),
            pltpu.VMEM((2, 2, ROWS, 2 * HS), BF16),
            pltpu.VMEM((2, 2, ROWS, 2 * HS), BF16),
            pltpu.VMEM((2, HD, HALF), BF16),
            pltpu.VMEM((2, 2, 208, HALF), BF16),
            pltpu.VMEM((2, 2, 416, HALF), BF16),
            pltpu.VMEM((432, HALF), F32),
            pltpu.VMEM((2, 4, 2, 64, HALF), BF16),
            pltpu.VMEM((2, 3, 2, 64, HALF), BF16),
            pltpu.VMEM((8, 64, 512), BF16),
            pltpu.VMEM((8, 64, 512), BF16),
            pltpu.SemaphoreType.DMA((2,)),
            pltpu.SemaphoreType.DMA((N_COPIES,)),
            pltpu.SemaphoreType.DMA((N_COPIES,)),
            pltpu.SemaphoreType.DMA((8,)),
            pltpu.SemaphoreType.DMA((8,)),
        ] + edge + edge,
        compiler_params=pltpu.CompilerParams(
            collective_id=0, has_side_effects=True, vmem_limit_bytes=63 * 1024 * 1024
        ),
        cost_estimate=pl.CostEstimate(flops=12_100_000_000, bytes_accessed=25_000_000, transcendentals=2_600_000),
        name="attention_and_projection",
    )(queries[0], keys[0], values[0], grad_out[0], out_weight, frame_clip)
    return (res[None], dq[None], dk[None], dv[None], gw[:52, :BLOCK])


def solution(mesh):
    in_specs = (
        P("dp", "tm", None),
        P("dp", "tm", None),
        P("dp", "tm", None),
        P("dp", "tm", None),
        P(None, "dp"),
        P("dp", None),
    )
    out_specs = (
        P("dp", "tm", None),
        P("dp", "tm", None),
        P("dp", "tm", None),
        P("dp", "tm", None),
        P("tm", "dp"),
    )
    return jax.shard_map(
        on_device, mesh=mesh, in_specs=in_specs, out_specs=out_specs, check_vma=False
    )
```

```python
import functools
import math

import jax
import jax.numpy as jnp
from jax import lax
from jax.experimental import pallas as pl
from jax.experimental.pallas import tpu as pltpu
from jax.sharding import PartitionSpec as P

HS = 128
ROWS = 256
HD = 1664
HEADS = 13
BLOCK = 400
PIECE = 96
REST = 16
GROUPS = ((0, 3), (3, 6), (6, 9), (9, 11), (11, 13))
ORDER = (3, 4, 0, 1, 2)
HALF = 896
WIDE = 1664
MESH = pl.DeviceIdType.MESH
F32 = jnp.float32
BF16 = jnp.bfloat16
SCALE = HS ** (-0.5)
SCALE2 = SCALE * math.log2(math.e)


class Copies:
    def __init__(self, send, recv):
        self.send, self.recv, self.count = send, recv, 0
        self.started = []

    def start(self, src, dst, device):
        copy = pltpu.make_async_remote_copy(
            src_ref=src,
            dst_ref=dst,
            send_sem=self.send.at[self.count],
            recv_sem=self.recv.at[self.count],
            device_id=device,
            device_id_type=MESH,
        )
        self.count += 1
        copy.start()
        self.started.append(copy)
        return copy


def nt(a, b):
    return lax.dot_general(a, b, (((1,), (1,)), ((), ())), preferred_element_type=F32)


def tn(a, b):
    return lax.dot_general(a, b, (((0,), (0,)), ((), ())), preferred_element_type=F32)


def nn(a, b):
    return lax.dot_general(a, b, (((1,), (0,)), ((), ())), preferred_element_type=F32)


N_COPIES = 45


class Beside:
    def __init__(self, x, up, down, mid_up, mid_down, over_up, over_down, to_up, to_down, held, sems):
        self.x, self.up, self.down = x, up, down
        self.mid_up, self.mid_down = mid_up, mid_down
        self.over_up, self.over_down = over_up, over_down
        self.to_up, self.to_down, self.held = to_up, to_down, held
        self.send, self.recv, self.in_send, self.in_recv, self.on_send = sems

    def direct(self, group, which, way):
        first, last = GROUPS[group]
        lanes = pl.ds(first * HS, (last - first) * HS)
        src, dst = (self.to_up, self.to_down)[way](which, lanes)
        at = (group * 2 + which) * 2 + way
        return pltpu.make_async_remote_copy(
            src_ref=src, dst_ref=dst, send_sem=self.send.at[at], recv_sem=self.recv.at[at],
            device_id=(self.up, self.down)[way], device_id_type=MESH,
        )

    def into(self, group, which, way):
        first, last = GROUPS[group]
        lanes = pl.ds(first * HS, (last - first) * HS)
        src, _ = (self.to_up, self.to_down)[way](which, lanes)
        at = way * 2 + which
        return pltpu.make_async_remote_copy(
            src_ref=src, dst_ref=self.held.at[way, which], send_sem=self.in_send.at[at], recv_sem=self.in_recv.at[at],
            device_id=(self.mid_up, self.mid_down)[way][group - 3], device_id_type=MESH,
        )

    def onward(self, group, which, way):
        first, last = GROUPS[group]
        lanes = pl.ds(first * HS, (last - first) * HS)
        _, dst = (self.to_up, self.to_down)[way](which, lanes)
        return pltpu.make_async_remote_copy(
            src_ref=self.held.at[way, which], dst_ref=dst, send_sem=self.on_send.at[way * 2 + which],
            recv_sem=self.recv.at[(group * 2 + which) * 2 + way],
            device_id=(self.over_up, self.over_down)[way], device_id_type=MESH,
        )

    def inner(self, way):
        return self.x != (3, 0)[way]

    def start_inner(self, groups):
        for way in (0, 1):
            @pl.when(self.inner(way))
            def _():
                for group in groups:
                    for which in (0, 1):
                        self.direct(group, which, way).start()

    def start_into(self, group):
        for way in (0, 1):
            @pl.when(jnp.logical_not(self.inner(way)))
            def _():
                for which in (0, 1):
                    self.into(group, which, way).start()

    def start_over(self, groups):
        for way in (0, 1):
            @pl.when(jnp.logical_not(self.inner(way)))
            def _():
                for group in groups:
                    for which in (0, 1):
                        self.direct(group, which, way).start()

    def pass_on(self):
        for column in (1, 2):
            @pl.when(self.x == column)
            def _():
                for way in (0, 1):
                    group = 3 if (way == 0) == (column == 2) else 4
                    for which in (0, 1):
                        self.into(group, which, way).wait_recv()
                        self.onward(group, which, way).start()

    def wait(self, group):
        for way in (0, 1):
            for which in (0, 1):
                self.direct(group, which, way).wait_recv()

    def drain(self):
        for way in (0, 1):
            for which in (0, 1):
                for group in range(3):
                    self.direct(group, which, way).wait_send()

                @pl.when(self.inner(way))
                def _():
                    for group in (3, 4):
                        self.direct(group, which, way).wait_send()

                @pl.when(jnp.logical_not(self.inner(way)))
                def _():
                    for group in (3, 4):
                        self.into(group, which, way).wait_send()

                @pl.when(jnp.logical_or(self.x == 1, self.x == 2))
                def _():
                    self.onward(3, which, way).wait_send()


def body(
    q, k, v, go, weight, clip,
    res, dq, dk, dv, gw,
    kw, vw, w, bias, probs, mx, gm, gop, dsend, drecv, down, held_kv, held_grad,
    term, yr1, yr2, ysum, xs, xr, zs, zr,
    local, send, recv, z_send, z_recv, *edge_sems,
):
    tm = lax.axis_index("tm")
    dp = lax.axis_index("dp")
    x, zh, y = tm % 4, (tm // 4) % 2, tm // 8
    zl, c = dp // 2, dp % 2
    z = zh * 4 + zl

    def place(x_, y_, z_, c_):
        return ((y_ * 2 + z_ // 4) * 4 + x_, (z_ % 4) * 2 + c_)

    def in_row(x_, step):
        return (lax.rem(tm // 4 + 8 + step, 8) * 4 + x_, dp)

    up = (lax.rem(tm + 1, 32), dp)
    down_dev = (lax.rem(tm + 31, 32), dp)
    peer = place(x, y, z, 1 - c)
    along_x = [place(lax.rem(x + d, 4), y, z, c) for d in (1, 2, 3)]
    along_y = [place(x, lax.rem(y + d, 4), z, c) for d in (1, 2, 3)]
    along_z = [place(x, y, lax.rem(z + d, 8), c) for d in range(1, 8)]
    across_z = [place(x, y, lax.rem(z + d, 8), 1 - c) for d in range(1, 8)]
    step_free, step_full = 3 - 2 * zh, 1 + 2 * zh
    y_free, y_full = lax.rem(y + step_free, 4), lax.rem(y + step_full, 4)
    free, full = place(x, y_free, z, c), place(x, y_full, z, c)
    partners = [up, down_dev, peer] + along_x + along_y + along_z + across_z

    barrier = pltpu.get_barrier_semaphore()
    for device in partners:
        pl.semaphore_signal(barrier, inc=1, device_id=device, device_id_type=MESH)
    for column, step in ((0, -1), (3, 1)):
        @pl.when(x == column)
        def _():
            for column_ in (1, 2):
                pl.semaphore_signal(barrier, inc=1, device_id=in_row(column_, step), device_id_type=MESH)

    own_k = pltpu.make_async_copy(k, kw.at[pl.ds(ROWS, ROWS)], local.at[0])
    own_v = pltpu.make_async_copy(v, vw.at[pl.ds(ROWS, ROWS)], local.at[1])
    own_k.start()
    own_v.start()
    own = pl.ds(pl.multiple_of(dp * BLOCK, 16), BLOCK)
    own_w = pltpu.make_async_copy(weight, w.at[own], local.at[2])
    own_w.start()
    here = clip[0, tm]
    before_off = jnp.where(jnp.logical_and(tm > 0, clip[0, lax.rem(tm + 31, 32)] == here), 0.0, -1e30).astype(F32)
    after_off = jnp.where(jnp.logical_and(tm < 31, clip[0, lax.rem(tm + 1, 32)] == here), 0.0, -1e30).astype(F32)
    bias[:, pl.ds(0, ROWS)] = jnp.full((8, ROWS), before_off, F32)
    bias[:, pl.ds(ROWS, ROWS)] = jnp.zeros((8, ROWS), F32)
    bias[:, pl.ds(2 * ROWS, ROWS)] = jnp.full((8, ROWS), after_off, F32)

    copies = Copies(send, recv)
    mid = ((in_row(2, 0), in_row(1, 0)), (in_row(1, 0), in_row(2, 0)))
    over = (in_row(0, 1), in_row(3, -1))
    windows = (kw, vw)
    inputs = (k, v)
    keys_values = Beside(
        x, up, down_dev, *mid, *over,
        lambda which, lanes: (inputs[which].at[:, lanes], windows[which].at[pl.ds(0, ROWS), lanes]),
        lambda which, lanes: (inputs[which].at[:, lanes], windows[which].at[pl.ds(2 * ROWS, ROWS), lanes]),
        held_kv, edge_sems[:5],
    )
    grads = Beside(
        x, up, down_dev, *mid, *over,
        lambda which, lanes: (dsend.at[1, which, :, lanes], drecv.at[1, which, :, lanes]),
        lambda which, lanes: (dsend.at[0, which, :, lanes], drecv.at[0, which, :, lanes]),
        held_grad, edge_sems[5:],
    )
    pl.semaphore_wait(barrier, len(partners) + 2 * jnp.logical_or(x == 1, x == 2).astype(jnp.int32))

    def piece_at(block, at):
        return w.at[pl.ds(pl.multiple_of(block * BLOCK + at * PIECE, 16), PIECE)]

    def rest_at(block):
        return w.at[pl.ds(pl.multiple_of(block * BLOCK + 4 * PIECE, 16), REST)]

    def same(ref, device):
        return copies.start(ref, ref, device)

    w_z = []
    second = place(x, y, lax.rem(z + 2 + 4 * c, 8), c)
    for device in (along_z[0], along_z[6], second):
        mine = weight.at[pl.ds(pl.multiple_of(y * PIECE, 16), PIECE)]
        w_z.append(copies.start(mine, piece_at(dp, y), device))
        w_z.append(copies.start(weight.at[pl.ds(4 * PIECE, REST)], rest_at(dp), device))
    for group in (3, 4):
        keys_values.start_into(group)
    keys_values.start_inner(ORDER)
    w_peer = [copies.start(weight, w.at[own], peer)]
    go_peer = copies.start(go.at[:, pl.ds(pl.multiple_of(1536 * (1 - c), 128), WIDE)], gop, peer)

    others = [lax.rem(zl + d, 4) * 2 + c for d in (1, 2, 3)]
    for copy in w_z:
        copy.wait_recv()
    w_free = [same(piece_at(block, y), free) for block in others]
    w_full = [same(piece_at(block, y), full) for block in others]
    keys_values.start_over((0, 1, 2))
    for block in others:
        w_peer.append(same(piece_at(block, y), peer))
        w_peer.append(same(rest_at(block), peer))
    keys_values.pass_on()

    own_k.wait()
    own_v.wait()
    own_w.wait()

    def forward(h, carry):
        lanes = pl.ds(pl.multiple_of(h * HS, HS), HS)
        s = nt(q[:, lanes], kw[:, lanes]) * SCALE2 + bias[0:1, :]
        e = jnp.exp2(s - jnp.max(s, axis=-1, keepdims=True))
        p = (e * (1.0 / jnp.sum(e, axis=-1, keepdims=True))).astype(BF16)
        probs[h] = p
        mx[0, :, lanes] = nn(p, vw[:, lanes]).astype(BF16)
        return carry

    def w_arrived(sent, from_y):
        for block, copy in zip(others, sent):
            copy.wait_recv()
            w_peer.append(same(piece_at(block, from_y), peer))

    for index, group in enumerate(ORDER):
        if index == 2:
            w_free[0].wait_recv()
            w_free[1].wait_recv()
            w_free[2].wait_recv()
            w_on = [same(piece_at(block, y_full), free) for block in others]
            for block in others:
                w_peer.append(same(piece_at(block, y_full), peer))
        if index == 4:
            w_arrived(w_full, y_free)
            w_arrived(w_on, lax.rem(y + 2, 4))
        keys_values.wait(group)
        lax.fori_loop(*GROUPS[group], forward, 0)
    mx_peer = copies.start(mx.at[0], mx.at[1], peer)

    go_peer.wait_recv()
    mx_peer.wait_recv()

    def chunk(p, at):
        return term.at[p, pl.ds(pl.multiple_of(at * 416, 16), 416)]

    y_first, y_second, x_copies = [], [], []
    for p in (0, 1):
        def weight_term(h, carry):
            lanes = pl.ds(pl.multiple_of(h * HS, HS), HS)
            columns = pl.ds(pl.multiple_of(1536 * c + 768 * p, 128), HALF)
            term[p, lanes, :] = (
                tn(mx[0, :, lanes], go[:, columns]) + tn(mx[1, :, lanes], gop[:, 768 * p : 768 * p + HALF])
            ).astype(BF16)
            return carry

        lax.fori_loop(0, HEADS, weight_term, 0)
        y_first.append(copies.start(chunk(p, lax.rem(y + 2, 4)), yr1.at[p], free))
        y_second.append([copies.start(chunk(p, y_full), yr2.at[p, 1], full)])

    def y_next(p):
        y_first[p].wait_recv()
        part = chunk(p, y_free)
        part[...] = (part[...].astype(F32) + yr1[p].astype(F32)).astype(BF16)
        y_second[p].append(copies.start(part, yr2.at[p, 0], free))

    for copy in w_peer:
        copy.wait_recv()

    def backward(h, carry):
        lanes = pl.ds(pl.multiple_of(h * HS, HS), HS)
        g = gm[:, lanes]
        p = probs[h]
        delta = jnp.sum(g.astype(F32) * mx[0, :, lanes].astype(F32), axis=-1, keepdims=True)
        ds = (p.astype(F32) * (nt(g, vw[:, lanes]) - delta)).astype(BF16)
        dq[:, lanes] = (nn(ds, kw[:, lanes]) * SCALE).astype(BF16)
        for which, grad in ((0, tn(ds, q[:, lanes]) * SCALE), (1, tn(p, g))):
            dsend[0, which, :, lanes] = grad[:ROWS].astype(BF16)
            down[which, :, lanes] = grad[ROWS : 2 * ROWS]
            dsend[1, which, :, lanes] = grad[2 * ROWS :].astype(BF16)
        return carry

    for index, group in enumerate(ORDER):
        first, last = GROUPS[group]
        lanes = pl.ds(first * HS, (last - first) * HS)
        gm[:, lanes] = nn(go[...], w[:, lanes]).astype(BF16)
        lax.fori_loop(first, last, backward, 0)
        if group > 2:
            grads.start_into(group)
        else:
            grads.start_over((group,))
        grads.start_inner((group,))
        if index == 4:
            y_next(0)

    for i in range(5):
        columns = pl.ds(i * 640, 640)
        res[:, columns] = nt(mx[0], w[columns, :]).astype(BF16)
    y_next(1)
    grads.pass_on()

    for p in (0, 1):
        for copy in y_second[p]:
            copy.wait_recv()
        ysum[pl.ds(0, 416), :] = (
            chunk(p, y)[...].astype(F32) + yr2[p, 0].astype(F32) + yr2[p, 1].astype(F32)
        )
        ysum[pl.ds(416, 16), :] = jnp.zeros((16, HALF), F32)
        for to in range(4):
            for half in range(2):
                xs[p, to, half] = ysum[pl.ds(208 * half + 52 * to, 64), :].astype(BF16)
        x_copies.append([
            copies.start(xs.at[p, lax.rem(x + d, 4)], xr.at[p, d - 1], along_x[d - 1]) for d in (1, 2, 3)
        ])

    def to_owner(p, half, b):
        at = p * 4 + half * 2 + b
        z_to = half * 4 + c * 2 + p
        slot = lax.rem(z + 8 - z_to, 8)
        mine = jnp.logical_and(z_to == z, c == b)
        return mine, at, pltpu.make_async_remote_copy(
            src_ref=zs.at[at], dst_ref=zr.at[slot], send_sem=z_send.at[at], recv_sem=z_recv.at[slot],
            device_id=place(x, y, z_to, b), device_id_type=MESH,
        )

    for p in (0, 1):
        for copy in x_copies[p]:
            copy.wait_recv()
        for half in range(2):
            total = xs[p, x, half].astype(F32)
            for i in range(3):
                total = total + xr[p, i, half].astype(F32)
            for b in (0, 1):
                shift = lax.rem(2 * HALF - BLOCK * b - 32 * p - 64 * c, HALF)
                zs[p * 4 + half * 2 + b] = pltpu.roll(total, shift, 1)[:, :512].astype(BF16)
        for half in range(2):
            for b in (0, 1):
                mine, at, copy = to_owner(p, half, b)

                @pl.when(mine)
                def _():
                    zr[0] = zs[at]

                @pl.when(jnp.logical_not(mine))
                def _():
                    copy.start()

    def from_z(slot):
        return pltpu.make_async_remote_copy(
            src_ref=zs.at[0], dst_ref=zr.at[slot], send_sem=z_send.at[0], recv_sem=z_recv.at[slot],
            device_id=peer, device_id_type=MESH,
        )

    for slot in range(1, 8):
        from_z(slot).wait_recv()

    @pl.when(zl // 2 != c)
    def _():
        from_z(0).wait_recv()

    total = zr[0].astype(F32)
    for i in range(1, 8):
        total = total + zr[i].astype(F32)
    gw[...] = total.astype(BF16)

    for group in ORDER:
        first, last = GROUPS[group]
        lanes = pl.ds(first * HS, (last - first) * HS)
        grads.wait(group)
        for which, out in ((0, dk), (1, dv)):
            out[:, lanes] = (
                down[which, :, lanes]
                + drecv[0, which, :, lanes].astype(F32)
                + drecv[1, which, :, lanes].astype(F32)
            ).astype(BF16)
    for copy in copies.started:
        copy.wait_send()
    keys_values.drain()
    grads.drain()
    for p in (0, 1):
        for half in range(2):
            for b in (0, 1):
                mine, at, copy = to_owner(p, half, b)

                @pl.when(jnp.logical_not(mine))
                def _():
                    copy.wait_send()


def on_device(queries, keys, values, grad_out, out_weight, frame_clip):
    vmem = pl.BlockSpec(memory_space=pltpu.VMEM)
    hbm = pl.BlockSpec(memory_space=pl.ANY)
    half = jax.ShapeDtypeStruct((ROWS, HD), BF16)
    edge = [pltpu.SemaphoreType.DMA((n,)) for n in (20, 20, 4, 4, 4)]
    res, dq, dk, dv, gw = pl.pallas_call(
        body,
        out_shape=(
            jax.ShapeDtypeStruct((ROWS, 8 * BLOCK), BF16),
            half,
            half,
            half,
            jax.ShapeDtypeStruct((64, 512), BF16),
        ),
        in_specs=[vmem, hbm, hbm, vmem, hbm, pl.BlockSpec(memory_space=pltpu.SMEM)],
        out_specs=(vmem,) * 5,
        scratch_shapes=[
            pltpu.VMEM((3 * ROWS, HD), BF16),
            pltpu.VMEM((3 * ROWS, HD), BF16),
            pltpu.VMEM((8 * BLOCK, HD), BF16),
            pltpu.VMEM((8, 3 * ROWS), F32),
            pltpu.VMEM((HEADS, ROWS, 3 * ROWS), BF16),
            pltpu.VMEM((2, ROWS, HD), BF16),
            pltpu.VMEM((ROWS, HD), BF16),
            pltpu.VMEM((ROWS, WIDE), BF16),
            pltpu.VMEM((2, 2, ROWS, HD), BF16),
            pltpu.VMEM((2, 2, ROWS, HD), BF16),
            pltpu.VMEM((2, ROWS, HD), F32),
            pltpu.VMEM((2, 2, ROWS, 2 * HS), BF16),
            pltpu.VMEM((2, 2, ROWS, 2 * HS), BF16),
            pltpu.VMEM((2, HD, HALF), BF16),
            pltpu.VMEM((2, 416, HALF), BF16),
            pltpu.VMEM((2, 2, 416, HALF), BF16),
            pltpu.VMEM((432, HALF), F32),
            pltpu.VMEM((2, 4, 2, 64, HALF), BF16),
            pltpu.VMEM((2, 3, 2, 64, HALF), BF16),
            pltpu.VMEM((8, 64, 512), BF16),
            pltpu.VMEM((8, 64, 512), BF16),
            pltpu.SemaphoreType.DMA((3,)),
            pltpu.SemaphoreType.DMA((N_COPIES,)),
            pltpu.SemaphoreType.DMA((N_COPIES,)),
            pltpu.SemaphoreType.DMA((8,)),
            pltpu.SemaphoreType.DMA((8,)),
        ] + edge + edge,
        compiler_params=pltpu.CompilerParams(
            collective_id=0, has_side_effects=True, vmem_limit_bytes=63 * 1024 * 1024
        ),
        cost_estimate=pl.CostEstimate(flops=12_100_000_000, bytes_accessed=25_000_000, transcendentals=2_600_000),
        name="attention_and_projection",
    )(queries[0], keys[0], values[0], grad_out[0], out_weight.T, frame_clip)
    return (res[None], dq[None], dk[None], dv[None], gw[:52, :BLOCK])


def solution(mesh):
    in_specs = (
        P("dp", "tm", None),
        P("dp", "tm", None),
        P("dp", "tm", None),
        P("dp", "tm", None),
        P(None, "dp"),
        P("dp", None),
    )
    out_specs = (
        P("dp", "tm", None),
        P("dp", "tm", None),
        P("dp", "tm", None),
        P("dp", "tm", None),
        P("tm", "dp"),
    )
    return jax.shard_map(
        on_device, mesh=mesh, in_specs=in_specs, out_specs=out_specs, check_vma=False
    )
```

```python
import functools
import math

import jax
import jax.numpy as jnp
from jax import lax
from jax.experimental import pallas as pl
from jax.experimental.pallas import tpu as pltpu
from jax.sharding import PartitionSpec as P

HS = 128
ROWS = 256
HD = 1664
HEADS = 13
BLOCK = 400
PIECE = 96
REST = 16
GROUPS = ((0, 3), (3, 5), (5, 7), (7, 10), (10, 13))
ORDER = (3, 4, 0, 1, 2)
ARRIVAL = (0, 1, 3, 4, 2)
VIA = 3 * HS
LONG = 320
HALF = 896
WIDE = 1664
MESH = pl.DeviceIdType.MESH
F32 = jnp.float32
BF16 = jnp.bfloat16
SCALE = HS ** (-0.5)
SCALE2 = SCALE * math.log2(math.e)


class Copies:
    def __init__(self, send, recv):
        self.send, self.recv, self.count = send, recv, 0
        self.started = []

    def start(self, src, dst, device):
        copy = pltpu.make_async_remote_copy(
            src_ref=src,
            dst_ref=dst,
            send_sem=self.send.at[self.count],
            recv_sem=self.recv.at[self.count],
            device_id=device,
            device_id_type=MESH,
        )
        self.count += 1
        copy.start()
        self.started.append(copy)
        return copy


def nt(a, b):
    return lax.dot_general(a, b, (((1,), (1,)), ((), ())), preferred_element_type=F32)


def tn(a, b):
    return lax.dot_general(a, b, (((0,), (0,)), ((), ())), preferred_element_type=F32)


def nn(a, b):
    return lax.dot_general(a, b, (((1,), (0,)), ((), ())), preferred_element_type=F32)


N_COPIES = 52


class Beside:
    def __init__(self, x, up, down, mid_up, mid_down, over_up, over_down, to_up, to_down, held, sems):
        self.x, self.up, self.down = x, up, down
        self.mid_up, self.mid_down = mid_up, mid_down
        self.over_up, self.over_down = over_up, over_down
        self.to_up, self.to_down, self.held = to_up, to_down, held
        self.send, self.recv, self.in_send, self.in_recv, self.on_send = sems

    def direct(self, group, which, way):
        first, last = GROUPS[group]
        lanes = pl.ds(first * HS, (last - first) * HS)
        src, dst = (self.to_up, self.to_down)[way](which, lanes)
        at = (group * 2 + which) * 2 + way
        return pltpu.make_async_remote_copy(
            src_ref=src, dst_ref=dst, send_sem=self.send.at[at], recv_sem=self.recv.at[at],
            device_id=(self.up, self.down)[way], device_id_type=MESH,
        )

    def into(self, group, which, way):
        first, last = GROUPS[group]
        lanes = pl.ds(first * HS, (last - first) * HS)
        src, _ = (self.to_up, self.to_down)[way](which, lanes)
        at = way * 2 + which
        return pltpu.make_async_remote_copy(
            src_ref=src, dst_ref=self.held.at[way, which], send_sem=self.in_send.at[at], recv_sem=self.in_recv.at[at],
            device_id=(self.mid_up, self.mid_down)[way][group - 3], device_id_type=MESH,
        )

    def onward(self, group, which, way):
        first, last = GROUPS[group]
        lanes = pl.ds(first * HS, (last - first) * HS)
        _, dst = (self.to_up, self.to_down)[way](which, lanes)
        return pltpu.make_async_remote_copy(
            src_ref=self.held.at[way, which], dst_ref=dst, send_sem=self.on_send.at[way * 2 + which],
            recv_sem=self.recv.at[(group * 2 + which) * 2 + way],
            device_id=(self.over_up, self.over_down)[way], device_id_type=MESH,
        )

    def inner(self, way):
        return self.x != (3, 0)[way]

    def start_inner(self, groups):
        for way in (0, 1):
            @pl.when(self.inner(way))
            def _():
                for group in groups:
                    for which in (0, 1):
                        self.direct(group, which, way).start()

    def start_into(self, group):
        for way in (0, 1):
            @pl.when(jnp.logical_not(self.inner(way)))
            def _():
                for which in (0, 1):
                    self.into(group, which, way).start()

    def start_over(self, groups):
        for way in (0, 1):
            @pl.when(jnp.logical_not(self.inner(way)))
            def _():
                for group in groups:
                    for which in (0, 1):
                        self.direct(group, which, way).start()

    def pass_on(self):
        for column in (1, 2):
            @pl.when(self.x == column)
            def _():
                for way in (0, 1):
                    group = 3 if (way == 0) == (column == 2) else 4
                    for which in (0, 1):
                        self.into(group, which, way).wait_recv()
                        self.onward(group, which, way).start()

    def wait(self, group):
        for way in (0, 1):
            for which in (0, 1):
                self.direct(group, which, way).wait_recv()

    def drain(self):
        for way in (0, 1):
            for which in (0, 1):
                for group in range(3):
                    self.direct(group, which, way).wait_send()

                @pl.when(self.inner(way))
                def _():
                    for group in (3, 4):
                        self.direct(group, which, way).wait_send()

                @pl.when(jnp.logical_not(self.inner(way)))
                def _():
                    for group in (3, 4):
                        self.into(group, which, way).wait_send()

                @pl.when(jnp.logical_or(self.x == 1, self.x == 2))
                def _():
                    self.onward(3, which, way).wait_send()


def body(
    q, k, v, go, weight, clip,
    res, dq, dk, dv, gw,
    kw, vw, w, bias, probs, mx, gm, gop, dsend, drecv, down, held_kv, held_grad,
    term, yr1, yr2, ysum, xs, xr, zs, zr,
    local, send, recv, z_send, z_recv, *edge_sems,
):
    tm = lax.axis_index("tm")
    dp = lax.axis_index("dp")
    x, zh, y = tm % 4, (tm // 4) % 2, tm // 8
    zl, c = dp // 2, dp % 2
    z = zh * 4 + zl

    def place(x_, y_, z_, c_):
        return ((y_ * 2 + z_ // 4) * 4 + x_, (z_ % 4) * 2 + c_)

    def in_row(x_, step):
        return (lax.rem(tm // 4 + 8 + step, 8) * 4 + x_, dp)

    up = (lax.rem(tm + 1, 32), dp)
    down_dev = (lax.rem(tm + 31, 32), dp)
    peer = place(x, y, z, 1 - c)
    along_x = [place(lax.rem(x + d, 4), y, z, c) for d in (1, 2, 3)]
    along_y = [place(x, lax.rem(y + d, 4), z, c) for d in (1, 2, 3)]
    along_z = [place(x, y, lax.rem(z + d, 8), c) for d in range(1, 8)]
    across_z = [place(x, y, lax.rem(z + d, 8), 1 - c) for d in range(1, 8)]
    step_free, step_full = 3 - 2 * zh, 1 + 2 * zh
    y_free, y_full = lax.rem(y + step_free, 4), lax.rem(y + step_full, 4)
    free, full = place(x, y_free, z, c), place(x, y_full, z, c)
    partners = [up, down_dev, peer] + along_x + along_y + along_z + across_z

    barrier = pltpu.get_barrier_semaphore()
    for device in partners:
        pl.semaphore_signal(barrier, inc=1, device_id=device, device_id_type=MESH)
    for column, step in ((0, -1), (3, 1)):
        @pl.when(x == column)
        def _():
            for column_ in (1, 2):
                pl.semaphore_signal(barrier, inc=1, device_id=in_row(column_, step), device_id_type=MESH)

    own_k = pltpu.make_async_copy(k, kw.at[pl.ds(ROWS, ROWS)], local.at[0])
    own_v = pltpu.make_async_copy(v, vw.at[pl.ds(ROWS, ROWS)], local.at[1])
    own_k.start()
    own_v.start()
    own = pl.ds(pl.multiple_of(dp * BLOCK, 16), BLOCK)
    own_w = pltpu.make_async_copy(weight, w.at[own], local.at[2])
    own_w.start()
    here = clip[0, tm]
    before_off = jnp.where(jnp.logical_and(tm > 0, clip[0, lax.rem(tm + 31, 32)] == here), 0.0, -1e30).astype(F32)
    after_off = jnp.where(jnp.logical_and(tm < 31, clip[0, lax.rem(tm + 1, 32)] == here), 0.0, -1e30).astype(F32)
    bias[:, pl.ds(0, ROWS)] = jnp.full((8, ROWS), before_off, F32)
    bias[:, pl.ds(ROWS, ROWS)] = jnp.zeros((8, ROWS), F32)
    bias[:, pl.ds(2 * ROWS, ROWS)] = jnp.full((8, ROWS), after_off, F32)

    copies = Copies(send, recv)
    mid = ((in_row(2, 0), in_row(1, 0)), (in_row(1, 0), in_row(2, 0)))
    over = (in_row(0, 1), in_row(3, -1))
    windows = (kw, vw)
    inputs = (k, v)
    keys_values = Beside(
        x, up, down_dev, *mid, *over,
        lambda which, lanes: (inputs[which].at[:, lanes], windows[which].at[pl.ds(0, ROWS), lanes]),
        lambda which, lanes: (inputs[which].at[:, lanes], windows[which].at[pl.ds(2 * ROWS, ROWS), lanes]),
        held_kv, edge_sems[:5],
    )
    grads = Beside(
        x, up, down_dev, *mid, *over,
        lambda which, lanes: (dsend.at[1, which, :, lanes], drecv.at[1, which, :, lanes]),
        lambda which, lanes: (dsend.at[0, which, :, lanes], drecv.at[0, which, :, lanes]),
        held_grad, edge_sems[5:],
    )
    pl.semaphore_wait(barrier, len(partners) + 2 * jnp.logical_or(x == 1, x == 2).astype(jnp.int32))

    def piece_at(block, at):
        return w.at[pl.ds(pl.multiple_of(block * BLOCK + at * PIECE, 16), PIECE)]

    def rest_at(block):
        return w.at[pl.ds(pl.multiple_of(block * BLOCK + 4 * PIECE, 16), REST)]

    def same(ref, device):
        return copies.start(ref, ref, device)

    w_z = []
    second = place(x, y, lax.rem(z + 2 + 4 * c, 8), c)
    for device in (along_z[0], along_z[6], second):
        mine = weight.at[pl.ds(pl.multiple_of(y * PIECE, 16), PIECE)]
        w_z.append(copies.start(mine, piece_at(dp, y), device))
        w_z.append(copies.start(weight.at[pl.ds(4 * PIECE, REST)], rest_at(dp), device))
    for group in (3, 4):
        keys_values.start_into(group)
    keys_values.start_inner(ARRIVAL[:2])
    w_peer = [copies.start(weight, w.at[own], peer)]
    go_peer = copies.start(go.at[:, pl.ds(pl.multiple_of(1536 * (1 - c), 128), WIDE)], gop, peer)

    others = [lax.rem(zl + d, 4) * 2 + c for d in (1, 2, 3)]
    for copy in w_z:
        copy.wait_recv()
    w_free = [same(piece_at(block, y), free) for block in others]
    w_full = [same(piece_at(block, y), full) for block in others]
    keys_values.start_over((0, 1, 2))
    keys_values.start_inner(ARRIVAL[2:])
    for block in others:
        w_peer.append(same(piece_at(block, y), peer))
        w_peer.append(same(rest_at(block), peer))
    keys_values.pass_on()

    own_k.wait()
    own_v.wait()
    own_w.wait()

    def forward(h, carry):
        lanes = pl.ds(pl.multiple_of(h * HS, HS), HS)
        s = nt(q[:, lanes], kw[:, lanes]) * SCALE2 + bias[0:1, :]
        e = jnp.exp2(s - jnp.max(s, axis=-1, keepdims=True))
        p = (e * (1.0 / jnp.sum(e, axis=-1, keepdims=True))).astype(BF16)
        probs[h] = p
        mx[0, :, lanes] = nn(p, vw[:, lanes]).astype(BF16)
        return carry

    def w_arrived(blocks, sent, from_y):
        for block, copy in zip(blocks, sent):
            copy.wait_recv()
            w_peer.append(same(piece_at(block, from_y), peer))

    for index, group in enumerate(ARRIVAL):
        if index == 1:
            w_on = []
            for i, (block, copy) in enumerate(zip(others, w_free)):
                copy.wait_recv()
                if i < 2:
                    w_on.append(same(piece_at(block, y_full), free))
            w_full[2].wait_recv()
            w_on.append(same(piece_at(others[2], y_free), full))
            for block in others:
                w_peer.append(same(piece_at(block, y_full), peer))
            w_peer.append(same(piece_at(others[2], y_free), peer))
        if index == 4:
            w_arrived(others[:2], w_full[:2], y_free)
            w_arrived(others, w_on, lax.rem(y + 2, 4))
        keys_values.wait(group)
        lax.fori_loop(*GROUPS[group], forward, 0)
    mx_peer = copies.start(mx.at[0], mx.at[1], peer)

    go_peer.wait_recv()
    mx_peer.wait_recv()

    def chunk(p, at):
        return term.at[p, pl.ds(pl.multiple_of(at * 416, 16), 416)]

    def near(p, at):
        return term.at[p, pl.ds(pl.multiple_of(at * 416, 16), LONG)]

    def far(p, at):
        return term.at[p, pl.ds(pl.multiple_of(at * 416 + LONG, 16), 416 - LONG)]

    opposite = lax.rem(y + 2, 4)
    y_first, y_second, x_copies = [], [], []
    for p in (0, 1):
        def weight_term(h, carry):
            lanes = pl.ds(pl.multiple_of(h * HS, HS), HS)
            columns = pl.ds(pl.multiple_of(1536 * c + 768 * p, 128), HALF)
            term[p, lanes, :] = (
                tn(mx[0, :, lanes], go[:, columns]) + tn(mx[1, :, lanes], gop[:, 768 * p : 768 * p + HALF])
            ).astype(BF16)
            return carry

        lax.fori_loop(0, HEADS, weight_term, 0)
        y_first.append((
            copies.start(near(p, opposite), yr1.at[p, pl.ds(0, LONG)], free),
            copies.start(far(p, opposite), yr1.at[p, pl.ds(LONG, 416 - LONG)], full),
        ))
        y_second.append([
            copies.start(near(p, y_full), yr2.at[p, 1, pl.ds(0, LONG)], full),
            copies.start(far(p, y_free), yr2.at[p, 0, pl.ds(LONG, 416 - LONG)], free),
        ])

    def y_next(p):
        for copy, part, rows, side, device in (
            (y_first[p][1], far(p, y_full), pl.ds(LONG, 416 - LONG), 1, full),
            (y_first[p][0], near(p, y_free), pl.ds(0, LONG), 0, free),
        ):
            copy.wait_recv()
            part[...] = (part[...].astype(F32) + yr1[p, rows].astype(F32)).astype(BF16)
            y_second[p].append(copies.start(part, yr2.at[p, side, rows], device))

    for copy in w_peer:
        copy.wait_recv()

    def backward(h, carry):
        lanes = pl.ds(pl.multiple_of(h * HS, HS), HS)
        g = gm[:, lanes]
        p = probs[h]
        delta = jnp.sum(g.astype(F32) * mx[0, :, lanes].astype(F32), axis=-1, keepdims=True)
        ds = (p.astype(F32) * (nt(g, vw[:, lanes]) - delta)).astype(BF16)
        dq[:, lanes] = (nn(ds, kw[:, lanes]) * SCALE).astype(BF16)
        for which, grad in ((0, tn(ds, q[:, lanes]) * SCALE), (1, tn(p, g))):
            dsend[0, which, :, lanes] = grad[:ROWS].astype(BF16)
            down[which, :, lanes] = grad[ROWS : 2 * ROWS]
            dsend[1, which, :, lanes] = grad[2 * ROWS :].astype(BF16)
        return carry

    for index, group in enumerate(ORDER):
        first, last = GROUPS[group]
        lanes = pl.ds(first * HS, (last - first) * HS)
        gm[:, lanes] = nn(go[...], w[:, lanes]).astype(BF16)
        lax.fori_loop(first, last, backward, 0)
        if group > 2:
            grads.start_into(group)
        else:
            grads.start_over((group,))
        grads.start_inner((group,))
        if index == 4:
            y_next(0)

    for i in range(5):
        columns = pl.ds(i * 640, 640)
        res[:, columns] = nt(mx[0], w[columns, :]).astype(BF16)
    y_next(1)
    grads.pass_on()

    for p in (0, 1):
        for copy in y_second[p]:
            copy.wait_recv()
        ysum[pl.ds(0, 416), :] = (
            chunk(p, y)[...].astype(F32) + yr2[p, 0].astype(F32) + yr2[p, 1].astype(F32)
        )
        ysum[pl.ds(416, 16), :] = jnp.zeros((16, HALF), F32)
        for to in range(4):
            for half in range(2):
                xs[p, to, half] = ysum[pl.ds(208 * half + 52 * to, 64), :].astype(BF16)
        x_copies.append([
            copies.start(xs.at[p, lax.rem(x + d, 4)], xr.at[p, d - 1], along_x[d - 1]) for d in (1, 2, 3)
        ])

    def add_beside(group):
        first, last = GROUPS[group]
        lanes = pl.ds(first * HS, (last - first) * HS)
        grads.wait(group)
        for which, out in ((0, dk), (1, dv)):
            out[:, lanes] = (
                down[which, :, lanes]
                + drecv[0, which, :, lanes].astype(F32)
                + drecv[1, which, :, lanes].astype(F32)
            ).astype(BF16)

    def to_owner(p, half, b):
        at = p * 4 + half * 2 + b
        z_to = half * 4 + c * 2 + p
        slot = lax.rem(z + 8 - z_to, 8)
        mine = jnp.logical_and(z_to == z, c == b)
        return mine, at, pltpu.make_async_remote_copy(
            src_ref=zs.at[at], dst_ref=zr.at[slot], send_sem=z_send.at[at], recv_sem=z_recv.at[slot],
            device_id=place(x, y, z_to, b), device_id_type=MESH,
        )

    for p in (0, 1):
        for copy in x_copies[p]:
            copy.wait_recv()
        for half in range(2):
            total = xs[p, x, half].astype(F32)
            for i in range(3):
                total = total + xr[p, i, half].astype(F32)
            for b in (0, 1):
                shift = lax.rem(2 * HALF - BLOCK * b - 32 * p - 64 * c, HALF)
                zs[p * 4 + half * 2 + b] = pltpu.roll(total, shift, 1)[:, :512].astype(BF16)
        for half in range(2):
            for b in (0, 1):
                mine, at, copy = to_owner(p, half, b)

                @pl.when(mine)
                def _():
                    zr[0] = zs[at]

                @pl.when(jnp.logical_not(mine))
                def _():
                    copy.start()

        for group in ((3, 4), (0, 1, 2))[p]:
            add_beside(group)

    def from_z(slot):
        return pltpu.make_async_remote_copy(
            src_ref=zs.at[0], dst_ref=zr.at[slot], send_sem=z_send.at[0], recv_sem=z_recv.at[slot],
            device_id=peer, device_id_type=MESH,
        )

    for slot in range(1, 8):
        from_z(slot).wait_recv()

    @pl.when(zl // 2 != c)
    def _():
        from_z(0).wait_recv()

    total = zr[0].astype(F32)
    for i in range(1, 8):
        total = total + zr[i].astype(F32)
    gw[...] = total[:52, :BLOCK].astype(BF16)

    for copy in copies.started:
        copy.wait_send()
    keys_values.drain()
    grads.drain()
    for p in (0, 1):
        for half in range(2):
            for b in (0, 1):
                mine, at, copy = to_owner(p, half, b)

                @pl.when(jnp.logical_not(mine))
                def _():
                    copy.wait_send()


PARTS = 4


def put_out(*refs):
    ins, outs, held = refs[:5], refs[5:10], refs[10:15]
    in_sem, out_sem = refs[15:]
    steps = []
    for i, (src, dst, via) in enumerate(zip(ins, outs, held)):
        parts = PARTS if i < 4 else 1
        rows = src.shape[0] // parts
        for j in range(parts):
            at = pl.ds(j * rows, rows)
            n = len(steps)
            a, b, c = (src, via, dst) if parts == 1 else (src.at[at], via.at[at], dst.at[at])
            steps.append((
                pltpu.make_async_copy(a, b, in_sem.at[n]),
                pltpu.make_async_copy(b, c, out_sem.at[n]),
            ))
    for first, _ in steps:
        first.start()
    for first, second in steps:
        first.wait()
        second.start()
    for _, second in steps:
        second.wait()


def on_device(queries, keys, values, grad_out, out_weight, frame_clip):
    vmem = pl.BlockSpec(memory_space=pltpu.VMEM)
    hbm = pl.BlockSpec(memory_space=pl.ANY)
    half = jax.ShapeDtypeStruct((ROWS, HD), BF16)
    edge = [pltpu.SemaphoreType.DMA((n,)) for n in (20, 20, 4, 4, 4)]
    res, dq, dk, dv, gw = pl.pallas_call(
        body,
        out_shape=(
            jax.ShapeDtypeStruct((ROWS, 8 * BLOCK), BF16),
            half,
            half,
            half,
            jax.ShapeDtypeStruct((52, BLOCK), BF16),
        ),
        in_specs=[vmem, hbm, hbm, vmem, hbm, pl.BlockSpec(memory_space=pltpu.SMEM)],
        out_specs=(vmem,) * 5,
        scratch_shapes=[
            pltpu.VMEM((3 * ROWS, HD), BF16),
            pltpu.VMEM((3 * ROWS, HD), BF16),
            pltpu.VMEM((8 * BLOCK, HD), BF16),
            pltpu.VMEM((8, 3 * ROWS), F32),
            pltpu.VMEM((HEADS, ROWS, 3 * ROWS), BF16),
            pltpu.VMEM((2, ROWS, HD), BF16),
            pltpu.VMEM((ROWS, HD), BF16),
            pltpu.VMEM((ROWS, WIDE), BF16),
            pltpu.VMEM((2, 2, ROWS, HD), BF16),
            pltpu.VMEM((2, 2, ROWS, HD), BF16),
            pltpu.VMEM((2, ROWS, HD), F32),
            pltpu.VMEM((2, 2, ROWS, VIA), BF16),
            pltpu.VMEM((2, 2, ROWS, VIA), BF16),
            pltpu.VMEM((2, HD, HALF), BF16),
            pltpu.VMEM((2, 416, HALF), BF16),
            pltpu.VMEM((2, 2, 416, HALF), BF16),
            pltpu.VMEM((432, HALF), F32),
            pltpu.VMEM((2, 4, 2, 64, HALF), BF16),
            pltpu.VMEM((2, 3, 2, 64, HALF), BF16),
            pltpu.VMEM((8, 64, 512), BF16),
            pltpu.VMEM((8, 64, 512), BF16),
            pltpu.SemaphoreType.DMA((3,)),
            pltpu.SemaphoreType.DMA((N_COPIES,)),
            pltpu.SemaphoreType.DMA((N_COPIES,)),
            pltpu.SemaphoreType.DMA((8,)),
            pltpu.SemaphoreType.DMA((8,)),
        ] + edge + edge,
        compiler_params=pltpu.CompilerParams(
            collective_id=0, has_side_effects=True, vmem_limit_bytes=63 * 1024 * 1024
        ),
        cost_estimate=pl.CostEstimate(flops=12_100_000_000, bytes_accessed=25_000_000, transcendentals=2_600_000),
        name="attention_and_projection",
    )(queries[0], keys[0], values[0], grad_out[0], out_weight.T, frame_clip)
    outs = (res, dq, dk, dv, gw)
    res, dq, dk, dv, gw = pl.pallas_call(
        put_out,
        out_shape=tuple(jax.ShapeDtypeStruct(a.shape, a.dtype) for a in outs),
        in_specs=[hbm] * 5,
        out_specs=(hbm,) * 5,
        scratch_shapes=[pltpu.VMEM(a.shape, a.dtype) for a in outs]
        + [pltpu.SemaphoreType.DMA((4 * PARTS + 1,)), pltpu.SemaphoreType.DMA((4 * PARTS + 1,))],
        compiler_params=pltpu.CompilerParams(vmem_limit_bytes=60 * 1024 * 1024),
        name="outputs",
    )(*outs)
    return (res[None], dq[None], dk[None], dv[None], gw)


def solution(mesh):
    in_specs = (
        P("dp", "tm", None),
        P("dp", "tm", None),
        P("dp", "tm", None),
        P("dp", "tm", None),
        P(None, "dp"),
        P("dp", None),
    )
    out_specs = (
        P("dp", "tm", None),
        P("dp", "tm", None),
        P("dp", "tm", None),
        P("dp", "tm", None),
        P("tm", "dp"),
    )
    return jax.shard_map(
        on_device, mesh=mesh, in_specs=in_specs, out_specs=out_specs, check_vma=False
    )
```

```python
import functools
import math

import jax
import jax.numpy as jnp
from jax import lax
from jax.experimental import pallas as pl
from jax.experimental.pallas import tpu as pltpu
from jax.sharding import PartitionSpec as P

HS = 128
ROWS = 256
HD = 1664
HEADS = 13
BLOCK = 400
PIECE = 96
REST = 16
GROUPS = ((6, 9), (3, 6), (0, 3), (9, 11), (11, 13))
ORDER = (3, 4, 0, 1, 2)
HALF = 896
WIDE = 1664
MESH = pl.DeviceIdType.MESH
F32 = jnp.float32
BF16 = jnp.bfloat16
SCALE = HS ** (-0.5)
SCALE2 = SCALE * math.log2(math.e)


class Copies:
    def __init__(self, send, recv):
        self.send, self.recv, self.count = send, recv, 0
        self.started = []

    def start(self, src, dst, device):
        copy = pltpu.make_async_remote_copy(
            src_ref=src,
            dst_ref=dst,
            send_sem=self.send.at[self.count],
            recv_sem=self.recv.at[self.count],
            device_id=device,
            device_id_type=MESH,
        )
        self.count += 1
        copy.start()
        self.started.append(copy)
        return copy


def nt(a, b):
    return lax.dot_general(a, b, (((1,), (1,)), ((), ())), preferred_element_type=F32)


def tn(a, b):
    return lax.dot_general(a, b, (((0,), (0,)), ((), ())), preferred_element_type=F32)


def nn(a, b):
    return lax.dot_general(a, b, (((1,), (0,)), ((), ())), preferred_element_type=F32)


N_COPIES = 42


class Beside:
    def __init__(self, x, up, down, mid_up, mid_down, over_up, over_down, to_up, to_down, held, sems):
        self.x, self.up, self.down = x, up, down
        self.mid_up, self.mid_down = mid_up, mid_down
        self.over_up, self.over_down = over_up, over_down
        self.to_up, self.to_down, self.held = to_up, to_down, held
        self.send, self.recv, self.in_send, self.in_recv, self.on_send = sems

    def direct(self, group, which, way):
        first, last = GROUPS[group]
        lanes = pl.ds(first * HS, (last - first) * HS)
        src, dst = (self.to_up, self.to_down)[way](which, lanes)
        at = (group * 2 + which) * 2 + way
        return pltpu.make_async_remote_copy(
            src_ref=src, dst_ref=dst, send_sem=self.send.at[at], recv_sem=self.recv.at[at],
            device_id=(self.up, self.down)[way], device_id_type=MESH,
        )

    def into(self, group, which, way):
        first, last = GROUPS[group]
        lanes = pl.ds(first * HS, (last - first) * HS)
        src, _ = (self.to_up, self.to_down)[way](which, lanes)
        at = way * 2 + which
        return pltpu.make_async_remote_copy(
            src_ref=src, dst_ref=self.held.at[way, which], send_sem=self.in_send.at[at], recv_sem=self.in_recv.at[at],
            device_id=(self.mid_up, self.mid_down)[way][group - 3], device_id_type=MESH,
        )

    def onward(self, group, which, way):
        first, last = GROUPS[group]
        lanes = pl.ds(first * HS, (last - first) * HS)
        _, dst = (self.to_up, self.to_down)[way](which, lanes)
        return pltpu.make_async_remote_copy(
            src_ref=self.held.at[way, which], dst_ref=dst, send_sem=self.on_send.at[way * 2 + which],
            recv_sem=self.recv.at[(group * 2 + which) * 2 + way],
            device_id=(self.over_up, self.over_down)[way], device_id_type=MESH,
        )

    def inner(self, way):
        return self.x != (3, 0)[way]

    def start_inner(self, groups):
        for way in (0, 1):
            @pl.when(self.inner(way))
            def _():
                for group in groups:
                    for which in (0, 1):
                        self.direct(group, which, way).start()

    def start_into(self, group):
        for way in (0, 1):
            @pl.when(jnp.logical_not(self.inner(way)))
            def _():
                for which in (0, 1):
                    self.into(group, which, way).start()

    def start_over(self, groups):
        for way in (0, 1):
            @pl.when(jnp.logical_not(self.inner(way)))
            def _():
                for group in groups:
                    for which in (0, 1):
                        self.direct(group, which, way).start()

    def pass_on(self):
        for column in (1, 2):
            @pl.when(self.x == column)
            def _():
                for way in (0, 1):
                    group = 3 if (way == 0) == (column == 2) else 4
                    for which in (0, 1):
                        self.into(group, which, way).wait_recv()
                        self.onward(group, which, way).start()

    def wait(self, group):
        for way in (0, 1):
            for which in (0, 1):
                self.direct(group, which, way).wait_recv()

    def drain(self):
        for way in (0, 1):
            for which in (0, 1):
                for group in range(3):
                    self.direct(group, which, way).wait_send()

                @pl.when(self.inner(way))
                def _():
                    for group in (3, 4):
                        self.direct(group, which, way).wait_send()

                @pl.when(jnp.logical_not(self.inner(way)))
                def _():
                    for group in (3, 4):
                        self.into(group, which, way).wait_send()

                @pl.when(jnp.logical_or(self.x == 1, self.x == 2))
                def _():
                    self.onward(3, which, way).wait_send()


def body(
    q, k, v, go, weight, clip,
    res, dq, dk, dv, gw,
    kw, vw, w, bias, probs, mx, mxs, gm, gos, dsend, drecv, down, held_kv, held_grad,
    term, yr, ysum, xs, xr, zs, zr,
    local, send, recv, z_send, z_recv, mx_send, mx_recv, *edge_sems,
):
    tm = lax.axis_index("tm")
    dp = lax.axis_index("dp")
    x, zh, y = tm % 4, (tm // 4) % 2, tm // 8
    zl, c = dp // 2, dp % 2
    z = zh * 4 + zl

    def place(x_, y_, z_, c_):
        return ((y_ * 2 + z_ // 4) * 4 + x_, (z_ % 4) * 2 + c_)

    def in_row(x_, step):
        return (lax.rem(tm // 4 + 8 + step, 8) * 4 + x_, dp)

    up = (lax.rem(tm + 1, 32), dp)
    down_dev = (lax.rem(tm + 31, 32), dp)
    peer = place(x, y, z, 1 - c)
    along_x = [place(lax.rem(x + d, 4), y, z, c) for d in (1, 2, 3)]
    along_z = [place(x, y, lax.rem(z + d, 8), c) for d in (1, 2, 6, 7)]
    half_of = lax.rem((y + 1) // 2, 2)
    beside_y = y + 1 - 2 * (y % 2)
    beside, beside_peer = place(x, beside_y, z, c), place(x, beside_y, z, 1 - c)
    same_half = place(x, 3 - y, z, c)
    from_y = jnp.where(y % 2 == 0, 2 * (zl // 2), 3 - 2 * (zl // 2))
    from_c = y // 2
    own_part = jnp.logical_and(from_c == c, from_y == y)
    step_free, step_full = 3 - 2 * zh, 1 + 2 * zh
    y_free, y_full = lax.rem(y + step_free, 4), lax.rem(y + step_full, 4)
    free, full = place(x, y_free, z, c), place(x, y_full, z, c)
    partners = [up, down_dev, peer, free, full, beside_peer] + along_x + along_z

    barrier = pltpu.get_barrier_semaphore()
    for device in partners:
        pl.semaphore_signal(barrier, inc=1, device_id=device, device_id_type=MESH)
    for z_from in range(8):
        @pl.when(jnp.logical_not(jnp.logical_and(own_part, z_from == z)))
        def _():
            pl.semaphore_signal(barrier, inc=1, device_id=place(x, from_y, z_from, from_c), device_id_type=MESH)
    for column, step in ((0, -1), (3, 1)):
        @pl.when(x == column)
        def _():
            for column_ in (1, 2):
                pl.semaphore_signal(barrier, inc=1, device_id=in_row(column_, step), device_id_type=MESH)

    own_k = pltpu.make_async_copy(k, kw.at[pl.ds(ROWS, ROWS)], local.at[0])
    own_v = pltpu.make_async_copy(v, vw.at[pl.ds(ROWS, ROWS)], local.at[1])
    own_k.start()
    own_v.start()
    own = pl.ds(pl.multiple_of(dp * BLOCK, 16), BLOCK)
    own_w = pltpu.make_async_copy(weight, w.at[own], local.at[2])
    own_w.start()
    here = clip[0, tm]
    before_off = jnp.where(jnp.logical_and(tm > 0, clip[0, lax.rem(tm + 31, 32)] == here), 0.0, -1e30).astype(F32)
    after_off = jnp.where(jnp.logical_and(tm < 31, clip[0, lax.rem(tm + 1, 32)] == here), 0.0, -1e30).astype(F32)
    bias[:, pl.ds(0, ROWS)] = jnp.full((8, ROWS), before_off, F32)
    bias[:, pl.ds(ROWS, ROWS)] = jnp.zeros((8, ROWS), F32)
    bias[:, pl.ds(2 * ROWS, ROWS)] = jnp.full((8, ROWS), after_off, F32)

    copies = Copies(send, recv)
    mid = ((in_row(2, 0), in_row(1, 0)), (in_row(1, 0), in_row(2, 0)))
    over = (in_row(0, 1), in_row(3, -1))
    windows = (kw, vw)
    inputs = (k, v)
    keys_values = Beside(
        x, up, down_dev, *mid, *over,
        lambda which, lanes: (inputs[which].at[:, lanes], windows[which].at[pl.ds(0, ROWS), lanes]),
        lambda which, lanes: (inputs[which].at[:, lanes], windows[which].at[pl.ds(2 * ROWS, ROWS), lanes]),
        held_kv, edge_sems[:5],
    )
    grads = Beside(
        x, up, down_dev, *mid, *over,
        lambda which, lanes: (dsend.at[1, which, :, lanes], drecv.at[1, which, :, lanes]),
        lambda which, lanes: (dsend.at[0, which, :, lanes], drecv.at[0, which, :, lanes]),
        held_grad, edge_sems[5:],
    )
    signals = len(partners) + 8 - own_part.astype(jnp.int32) + 2 * jnp.logical_or(x == 1, x == 2).astype(jnp.int32)
    pl.semaphore_wait(barrier, signals)

    def piece_at(block, at):
        return w.at[pl.ds(pl.multiple_of(block * BLOCK + at * PIECE, 16), PIECE)]

    def rest_at(block):
        return w.at[pl.ds(pl.multiple_of(block * BLOCK + 4 * PIECE, 16), REST)]

    def same(ref, device):
        return copies.start(ref, ref, device)

    def go_half(which):
        return go.at[:, pl.ds(pl.multiple_of(1536 * which, 128), WIDE)]

    go_beside = copies.start(go_half(1 - half_of), gos.at[1], beside)
    w_z = []
    second = place(x, y, lax.rem(z + 2 + 4 * c, 8), c)
    for device in (along_z[0], along_z[3], second):
        mine = weight.at[pl.ds(pl.multiple_of(y * PIECE, 16), PIECE)]
        w_z.append(copies.start(mine, piece_at(dp, y), device))
        w_z.append(copies.start(weight.at[pl.ds(4 * PIECE, REST)], rest_at(dp), device))
    for group in (3, 4):
        keys_values.start_into(group)
    keys_values.start_inner(ORDER)
    w_peer = [copies.start(weight, w.at[own], peer)]
    go_peer = [copies.start(go_half(half_of), gos.at[0], peer)]

    others = [lax.rem(zl + d, 4) * 2 + c for d in (1, 2, 3)]
    for copy in w_z:
        copy.wait_recv()
    w_free = [same(piece_at(block, y), free) for block in others]
    w_full = [same(piece_at(block, y), full) for block in others]
    keys_values.start_over((0, 1, 2))
    for block in others:
        w_peer.append(same(piece_at(block, y), peer))
        w_peer.append(same(rest_at(block), peer))
    go_beside.wait_recv()
    go_peer.append(copies.start(gos.at[1], gos.at[2], peer))
    keys_values.pass_on()

    own_k.wait()
    own_v.wait()
    own_w.wait()

    def forward(h, carry):
        lanes = pl.ds(pl.multiple_of(h * HS, HS), HS)
        s = nt(q[:, lanes], kw[:, lanes]) * SCALE2 + bias[0:1, :]
        e = jnp.exp2(s - jnp.max(s, axis=-1, keepdims=True))
        p = (e * (1.0 / jnp.sum(e, axis=-1, keepdims=True))).astype(BF16)
        probs[h] = p
        mx[:, lanes] = nn(p, vw[:, lanes]).astype(BF16)
        return carry

    def mixed_to(window, part):
        first, size = ((384, 512), (0, 384))[part]
        src = mx.at[:, 768 * window + first : 768 * window + first + size]
        slot = jnp.where(c == window, 1, 2)
        here = pl.ds(first, size)
        at = (window * 2 + part) * 2
        return (
            pltpu.make_async_remote_copy(
                src_ref=src, dst_ref=mxs.at[slot, :, here], send_sem=mx_send.at[at], recv_sem=mx_recv.at[slot * 2 + part],
                device_id=place(x, beside_y, z, window), device_id_type=MESH),
            pltpu.make_async_remote_copy(
                src_ref=src, dst_ref=mxs.at[0, :, here], send_sem=mx_send.at[at + 1], recv_sem=mx_recv.at[part],
                device_id=peer, device_id_type=MESH),
        )

    def send_mixed(window, part):
        outside, inside = mixed_to(window, part)
        outside.start()

        @pl.when(c != window)
        def _():
            inside.start()

    def wait_mixed(slot, part):
        first, size = ((384, 512), (0, 384))[part]
        here = pl.ds(first, size)
        pltpu.make_async_remote_copy(
            src_ref=mx.at[:, here], dst_ref=mxs.at[slot, :, here], send_sem=mx_send.at[0], recv_sem=mx_recv.at[slot * 2 + part],
            device_id=peer, device_id_type=MESH).wait_recv()

    def w_arrived(sent, from_y):
        for block, copy in zip(others, sent):
            copy.wait_recv()
            w_peer.append(same(piece_at(block, from_y), peer))

    for index, group in enumerate(ORDER):
        if index == 2:
            w_free[0].wait_recv()
            w_free[1].wait_recv()
            w_free[2].wait_recv()
            w_on = [same(piece_at(block, y_full), free) for block in others]
            for block in others:
                w_peer.append(same(piece_at(block, y_full), peer))
        if index == 4:
            w_arrived(w_full, y_free)
            w_arrived(w_on, lax.rem(y + 2, 4))
        keys_values.wait(group)
        lax.fori_loop(*GROUPS[group], forward, 0)
        if index > 0:
            send_mixed(*((1, 0), (1, 1), (0, 0), (0, 1))[index - 1])

    for copy in go_peer:
        copy.wait_recv()
    for part in (0, 1):
        for slot in range(3):
            wait_mixed(slot, part)

    def chunk(p, parity):
        return term.at[p, pl.ds(pl.multiple_of(64 * c + 416 * parity, 16), 416)]

    y_copies, x_copies = [], []
    for p in (0, 1):
        def weight_term(h, carry):
            own_lanes = pl.ds(pl.multiple_of((6 * c + h) * HS, HS), HS)
            lanes = pl.ds(pl.multiple_of(h * HS, HS), HS)
            columns = pl.ds(pl.multiple_of(1536 * half_of + 768 * p, 128), HALF)
            total = tn(mx[:, own_lanes], go[:, columns])
            for i in range(3):
                total = total + tn(mxs[i, :, lanes], gos[i, :, 768 * p : 768 * p + HALF])
            term[p, lanes, :] = total.astype(BF16)
            return carry

        lax.fori_loop(0, 7, weight_term, 0)
        y_copies.append(copies.start(chunk(p, 1 - y % 2), yr.at[p], same_half))

    def sum_y(p):
        y_copies[p].wait_recv()
        ysum[pl.ds(0, 416), :] = chunk(p, y % 2)[...].astype(F32) + yr[p].astype(F32)
        ysum[pl.ds(416, 16), :] = jnp.zeros((16, HALF), F32)
        for to in range(4):
            for half in range(2):
                xs[p, to, half] = ysum[pl.ds(208 * half + 52 * to, 64), :].astype(BF16)
        x_copies.append([
            copies.start(xs.at[p, lax.rem(x + d, 4)], xr.at[p, d - 1], along_x[d - 1]) for d in (1, 2, 3)
        ])

    for copy in w_peer:
        copy.wait_recv()

    def backward(h, carry):
        lanes = pl.ds(pl.multiple_of(h * HS, HS), HS)
        g = gm[:, lanes]
        p = probs[h]
        delta = jnp.sum(g.astype(F32) * mx[:, lanes].astype(F32), axis=-1, keepdims=True)
        ds = (p.astype(F32) * (nt(g, vw[:, lanes]) - delta)).astype(BF16)
        dq[:, lanes] = (nn(ds, kw[:, lanes]) * SCALE).astype(BF16)
        for which, grad in ((0, tn(ds, q[:, lanes]) * SCALE), (1, tn(p, g))):
            dsend[0, which, :, lanes] = grad[:ROWS].astype(BF16)
            down[which, :, lanes] = grad[ROWS : 2 * ROWS]
            dsend[1, which, :, lanes] = grad[2 * ROWS :].astype(BF16)
        return carry

    for index, group in enumerate(ORDER):
        first, last = GROUPS[group]
        lanes = pl.ds(first * HS, (last - first) * HS)
        gm[:, lanes] = nn(go[...], w[:, lanes]).astype(BF16)
        lax.fori_loop(first, last, backward, 0)
        if group > 2:
            grads.start_into(group)
        else:
            grads.start_over((group,))
        grads.start_inner((group,))
        if index == 4:
            sum_y(0)

    for i in range(5):
        columns = pl.ds(i * 640, 640)
        res[:, columns] = nt(mx[...], w[columns, :]).astype(BF16)
    sum_y(1)
    grads.pass_on()

    def to_owner(p, half, b):
        at = p * 4 + half * 2 + b
        z_to = half * 4 + half_of * 2 + p
        slot = lax.rem(z + 8 - z_to, 8)
        y_to = 2 * c + y % 2
        mine = jnp.logical_and(jnp.logical_and(z_to == z, y_to == y), c == b)
        return mine, at, pltpu.make_async_remote_copy(
            src_ref=zs.at[at], dst_ref=zr.at[slot], send_sem=z_send.at[at], recv_sem=z_recv.at[slot],
            device_id=place(x, y_to, z_to, b), device_id_type=MESH,
        )

    for p in (0, 1):
        for copy in x_copies[p]:
            copy.wait_recv()
        for half in range(2):
            total = xs[p, x, half].astype(F32)
            for i in range(3):
                total = total + xr[p, i, half].astype(F32)
            for b in (0, 1):
                shift = lax.rem(2 * HALF - BLOCK * b - 32 * p - 64 * half_of, HALF)
                zs[p * 4 + half * 2 + b] = pltpu.roll(total, shift, 1)[:, :512].astype(BF16)
        for half in range(2):
            for b in (0, 1):
                mine, at, copy = to_owner(p, half, b)

                @pl.when(mine)
                def _():
                    zr[0] = zs[at]

                @pl.when(jnp.logical_not(mine))
                def _():
                    copy.start()

    def from_z(slot):
        return pltpu.make_async_remote_copy(
            src_ref=zs.at[0], dst_ref=zr.at[slot], send_sem=z_send.at[0], recv_sem=z_recv.at[slot],
            device_id=peer, device_id_type=MESH,
        )

    for group in ORDER:
        first, last = GROUPS[group]
        lanes = pl.ds(first * HS, (last - first) * HS)
        grads.wait(group)
        for which, out in ((0, dk), (1, dv)):
            out[:, lanes] = (
                down[which, :, lanes]
                + drecv[0, which, :, lanes].astype(F32)
                + drecv[1, which, :, lanes].astype(F32)
            ).astype(BF16)
    for slot in range(1, 8):
        from_z(slot).wait_recv()

    @pl.when(jnp.logical_not(own_part))
    def _():
        from_z(0).wait_recv()

    total = zr[0].astype(F32)
    for i in range(1, 8):
        total = total + zr[i].astype(F32)
    gw[...] = total[:52, :BLOCK].astype(BF16)

    for copy in copies.started:
        copy.wait_send()
    for window in (0, 1):
        for part in (0, 1):
            outside, inside = mixed_to(window, part)
            outside.wait_send()

            @pl.when(c != window)
            def _():
                inside.wait_send()

    keys_values.drain()
    grads.drain()
    for p in (0, 1):
        for half in range(2):
            for b in (0, 1):
                mine, at, copy = to_owner(p, half, b)

                @pl.when(jnp.logical_not(mine))
                def _():
                    copy.wait_send()


PARTS = 4


def put_out(*refs):
    ins, outs, held = refs[:5], refs[5:10], refs[10:15]
    in_sem, out_sem = refs[15:]
    steps = []
    for i, (src, dst, via) in enumerate(zip(ins, outs, held)):
        parts = PARTS if i < 4 else 1
        rows = src.shape[0] // parts
        for j in range(parts):
            at = pl.ds(j * rows, rows)
            n = len(steps)
            a, b, c = (src, via, dst) if parts == 1 else (src.at[at], via.at[at], dst.at[at])
            steps.append((
                pltpu.make_async_copy(a, b, in_sem.at[n]),
                pltpu.make_async_copy(b, c, out_sem.at[n]),
            ))
    for first, _ in steps:
        first.start()
    for first, second in steps:
        first.wait()
        second.start()
    for _, second in steps:
        second.wait()


def on_device(queries, keys, values, grad_out, out_weight, frame_clip):
    vmem = pl.BlockSpec(memory_space=pltpu.VMEM)
    hbm = pl.BlockSpec(memory_space=pl.ANY)
    half = jax.ShapeDtypeStruct((ROWS, HD), BF16)
    edge = [pltpu.SemaphoreType.DMA((n,)) for n in (20, 20, 4, 4, 4)]
    res, dq, dk, dv, gw = pl.pallas_call(
        body,
        out_shape=(
            jax.ShapeDtypeStruct((ROWS, 8 * BLOCK), BF16),
            half,
            half,
            half,
            jax.ShapeDtypeStruct((52, BLOCK), BF16),
        ),
        in_specs=[vmem, hbm, hbm, vmem, hbm, pl.BlockSpec(memory_space=pltpu.SMEM)],
        out_specs=(vmem,) * 5,
        scratch_shapes=[
            pltpu.VMEM((3 * ROWS, HD), BF16),
            pltpu.VMEM((3 * ROWS, HD), BF16),
            pltpu.VMEM((8 * BLOCK, HD), BF16),
            pltpu.VMEM((8, 3 * ROWS), F32),
            pltpu.VMEM((HEADS, ROWS, 3 * ROWS), BF16),
            pltpu.VMEM((ROWS, HD), BF16),
            pltpu.VMEM((3, ROWS, HALF), BF16),
            pltpu.VMEM((ROWS, HD), BF16),
            pltpu.VMEM((3, ROWS, WIDE), BF16),
            pltpu.VMEM((2, 2, ROWS, HD), BF16),
            pltpu.VMEM((2, 2, ROWS, HD), BF16),
            pltpu.VMEM((2, ROWS, HD), F32),
            pltpu.VMEM((2, 2, ROWS, 2 * HS), BF16),
            pltpu.VMEM((2, 2, ROWS, 2 * HS), BF16),
            pltpu.VMEM((2, HALF, HALF), BF16),
            pltpu.VMEM((2, 416, HALF), BF16),
            pltpu.VMEM((432, HALF), F32),
            pltpu.VMEM((2, 4, 2, 64, HALF), BF16),
            pltpu.VMEM((2, 3, 2, 64, HALF), BF16),
            pltpu.VMEM((8, 64, 512), BF16),
            pltpu.VMEM((8, 64, 512), BF16),
            pltpu.SemaphoreType.DMA((3,)),
            pltpu.SemaphoreType.DMA((N_COPIES,)),
            pltpu.SemaphoreType.DMA((N_COPIES,)),
            pltpu.SemaphoreType.DMA((8,)),
            pltpu.SemaphoreType.DMA((8,)),
            pltpu.SemaphoreType.DMA((8,)),
            pltpu.SemaphoreType.DMA((6,)),
        ] + edge + edge,
        compiler_params=pltpu.CompilerParams(
            collective_id=0, has_side_effects=True, vmem_limit_bytes=63 * 1024 * 1024
        ),
        cost_estimate=pl.CostEstimate(flops=12_100_000_000, bytes_accessed=25_000_000, transcendentals=2_600_000),
        name="attention_and_projection",
    )(queries[0], keys[0], values[0], grad_out[0], out_weight.T, frame_clip)
    outs = (res, dq, dk, dv, gw)
    res, dq, dk, dv, gw = pl.pallas_call(
        put_out,
        out_shape=tuple(jax.ShapeDtypeStruct(a.shape, a.dtype) for a in outs),
        in_specs=[hbm] * 5,
        out_specs=(hbm,) * 5,
        scratch_shapes=[pltpu.VMEM(a.shape, a.dtype) for a in outs]
        + [pltpu.SemaphoreType.DMA((4 * PARTS + 1,)), pltpu.SemaphoreType.DMA((4 * PARTS + 1,))],
        compiler_params=pltpu.CompilerParams(vmem_limit_bytes=60 * 1024 * 1024),
        name="outputs",
    )(*outs)
    return (res[None], dq[None], dk[None], dv[None], gw)


def solution(mesh):
    in_specs = (
        P("dp", "tm", None),
        P("dp", "tm", None),
        P("dp", "tm", None),
        P("dp", "tm", None),
        P(None, "dp"),
        P("dp", None),
    )
    out_specs = (
        P("dp", "tm", None),
        P("dp", "tm", None),
        P("dp", "tm", None),
        P("dp", "tm", None),
        P("tm", "dp"),
    )
    return jax.shard_map(
        on_device, mesh=mesh, in_specs=in_specs, out_specs=out_specs, check_vma=False
    )
```

```python
import functools
import math

import jax
import jax.numpy as jnp
from jax import lax
from jax.experimental import pallas as pl
from jax.experimental.pallas import tpu as pltpu
from jax.sharding import PartitionSpec as P

HS = 128
ROWS = 256
HD = 1664
HEADS = 13
BLOCK = 400
PIECE = 96
REST = 16
GROUPS = ((0, 3), (3, 6), (6, 9), (9, 11), (11, 13))
ORDER = (3, 4, 0, 1, 2)
HALF = 896
WIDTH = (896, 768)
WIDE = 1664
MESH = pl.DeviceIdType.MESH
F32 = jnp.float32
BF16 = jnp.bfloat16
SCALE = HS ** (-0.5)
SCALE2 = SCALE * math.log2(math.e)


class Copies:
    def __init__(self, send, recv):
        self.send, self.recv, self.count = send, recv, 0
        self.started = []

    def start(self, src, dst, device):
        copy = pltpu.make_async_remote_copy(
            src_ref=src,
            dst_ref=dst,
            send_sem=self.send.at[self.count],
            recv_sem=self.recv.at[self.count],
            device_id=device,
            device_id_type=MESH,
        )
        self.count += 1
        copy.start()
        self.started.append(copy)
        return copy


def nt(a, b):
    return lax.dot_general(a, b, (((1,), (1,)), ((), ())), preferred_element_type=F32)


def tn(a, b):
    return lax.dot_general(a, b, (((0,), (0,)), ((), ())), preferred_element_type=F32)


def nn(a, b):
    return lax.dot_general(a, b, (((1,), (0,)), ((), ())), preferred_element_type=F32)


N_COPIES = 45


class Beside:
    def __init__(self, x, up, down, mid_up, mid_down, over_up, over_down, to_up, to_down, held, sems):
        self.x, self.up, self.down = x, up, down
        self.mid_up, self.mid_down = mid_up, mid_down
        self.over_up, self.over_down = over_up, over_down
        self.to_up, self.to_down, self.held = to_up, to_down, held
        self.send, self.recv, self.in_send, self.in_recv, self.on_send = sems

    def direct(self, group, which, way):
        first, last = GROUPS[group]
        lanes = pl.ds(first * HS, (last - first) * HS)
        src, dst = (self.to_up, self.to_down)[way](which, lanes)
        at = (group * 2 + which) * 2 + way
        return pltpu.make_async_remote_copy(
            src_ref=src, dst_ref=dst, send_sem=self.send.at[at], recv_sem=self.recv.at[at],
            device_id=(self.up, self.down)[way], device_id_type=MESH,
        )

    def into(self, group, which, way):
        first, last = GROUPS[group]
        lanes = pl.ds(first * HS, (last - first) * HS)
        src, _ = (self.to_up, self.to_down)[way](which, lanes)
        at = way * 2 + which
        return pltpu.make_async_remote_copy(
            src_ref=src, dst_ref=self.held.at[way, which], send_sem=self.in_send.at[at], recv_sem=self.in_recv.at[at],
            device_id=(self.mid_up, self.mid_down)[way][group - 3], device_id_type=MESH,
        )

    def onward(self, group, which, way):
        first, last = GROUPS[group]
        lanes = pl.ds(first * HS, (last - first) * HS)
        _, dst = (self.to_up, self.to_down)[way](which, lanes)
        return pltpu.make_async_remote_copy(
            src_ref=self.held.at[way, which], dst_ref=dst, send_sem=self.on_send.at[way * 2 + which],
            recv_sem=self.recv.at[(group * 2 + which) * 2 + way],
            device_id=(self.over_up, self.over_down)[way], device_id_type=MESH,
        )

    def inner(self, way):
        return self.x != (3, 0)[way]

    def start_inner(self, groups):
        for way in (0, 1):
            @pl.when(self.inner(way))
            def _():
                for group in groups:
                    for which in (0, 1):
                        self.direct(group, which, way).start()

    def start_into(self, group):
        for way in (0, 1):
            @pl.when(jnp.logical_not(self.inner(way)))
            def _():
                for which in (0, 1):
                    self.into(group, which, way).start()

    def start_over(self, groups):
        for way in (0, 1):
            @pl.when(jnp.logical_not(self.inner(way)))
            def _():
                for group in groups:
                    for which in (0, 1):
                        self.direct(group, which, way).start()

    def pass_on(self):
        for column in (1, 2):
            @pl.when(self.x == column)
            def _():
                for way in (0, 1):
                    group = 3 if (way == 0) == (column == 2) else 4
                    for which in (0, 1):
                        self.into(group, which, way).wait_recv()
                        self.onward(group, which, way).start()

    def wait(self, group):
        for way in (0, 1):
            for which in (0, 1):
                self.direct(group, which, way).wait_recv()

    def drain(self):
        for way in (0, 1):
            for which in (0, 1):
                for group in range(3):
                    self.direct(group, which, way).wait_send()

                @pl.when(self.inner(way))
                def _():
                    for group in (3, 4):
                        self.direct(group, which, way).wait_send()

                @pl.when(jnp.logical_not(self.inner(way)))
                def _():
                    for group in (3, 4):
                        self.into(group, which, way).wait_send()

                @pl.when(jnp.logical_or(self.x == 1, self.x == 2))
                def _():
                    self.onward(3, which, way).wait_send()


def body(
    q, k, v, go, weight, clip,
    res, dq, dk, dv, gw,
    kw, vw, w, bias, probs, mx, gm, gop, dsend, drecv, down, held_kv, held_grad,
    term, yr1, yr2, ysum, edge, xs, xr, zs, zr,
    local, send, recv, z_send, z_recv, *edge_sems,
):
    tm = lax.axis_index("tm")
    dp = lax.axis_index("dp")
    x, zh, y = tm % 4, (tm // 4) % 2, tm // 8
    zl, c = dp // 2, dp % 2
    z = zh * 4 + zl

    def place(x_, y_, z_, c_):
        return ((y_ * 2 + z_ // 4) * 4 + x_, (z_ % 4) * 2 + c_)

    def in_row(x_, step):
        return (lax.rem(tm // 4 + 8 + step, 8) * 4 + x_, dp)

    up = (lax.rem(tm + 1, 32), dp)
    down_dev = (lax.rem(tm + 31, 32), dp)
    peer = place(x, y, z, 1 - c)
    along_x = [place(lax.rem(x + d, 4), y, z, c) for d in (1, 2, 3)]
    along_y = [place(x, lax.rem(y + d, 4), z, c) for d in (1, 2, 3)]
    along_z = [place(x, y, lax.rem(z + d, 8), c) for d in range(1, 8)]
    across_z = [place(x, y, lax.rem(z + d, 8), 1 - c) for d in range(1, 8)]
    step_free, step_full = 3 - 2 * zh, 1 + 2 * zh
    y_free, y_full = lax.rem(y + step_free, 4), lax.rem(y + step_full, 4)
    free, full = place(x, y_free, z, c), place(x, y_full, z, c)
    partners = [up, down_dev, peer] + along_x + along_y + along_z + across_z

    barrier = pltpu.get_barrier_semaphore()
    for device in partners:
        pl.semaphore_signal(barrier, inc=1, device_id=device, device_id_type=MESH)
    for column, step in ((0, -1), (3, 1)):
        @pl.when(x == column)
        def _():
            for column_ in (1, 2):
                pl.semaphore_signal(barrier, inc=1, device_id=in_row(column_, step), device_id_type=MESH)

    own_k = pltpu.make_async_copy(k, kw.at[pl.ds(ROWS, ROWS)], local.at[0])
    own_v = pltpu.make_async_copy(v, vw.at[pl.ds(ROWS, ROWS)], local.at[1])
    own_k.start()
    own_v.start()
    own = pl.ds(pl.multiple_of(dp * BLOCK, 16), BLOCK)
    own_w = pltpu.make_async_copy(weight, w.at[own], local.at[2])
    own_w.start()
    here = clip[0, tm]
    before_off = jnp.where(jnp.logical_and(tm > 0, clip[0, lax.rem(tm + 31, 32)] == here), 0.0, -1e30).astype(F32)
    after_off = jnp.where(jnp.logical_and(tm < 31, clip[0, lax.rem(tm + 1, 32)] == here), 0.0, -1e30).astype(F32)
    bias[:, pl.ds(0, ROWS)] = jnp.full((8, ROWS), before_off, F32)
    bias[:, pl.ds(ROWS, ROWS)] = jnp.zeros((8, ROWS), F32)
    bias[:, pl.ds(2 * ROWS, ROWS)] = jnp.full((8, ROWS), after_off, F32)

    copies = Copies(send, recv)
    mid = ((in_row(2, 0), in_row(1, 0)), (in_row(1, 0), in_row(2, 0)))
    over = (in_row(0, 1), in_row(3, -1))
    windows = (kw, vw)
    inputs = (k, v)
    keys_values = Beside(
        x, up, down_dev, *mid, *over,
        lambda which, lanes: (inputs[which].at[:, lanes], windows[which].at[pl.ds(0, ROWS), lanes]),
        lambda which, lanes: (inputs[which].at[:, lanes], windows[which].at[pl.ds(2 * ROWS, ROWS), lanes]),
        held_kv, edge_sems[:5],
    )
    grads = Beside(
        x, up, down_dev, *mid, *over,
        lambda which, lanes: (dsend.at[1, which, :, lanes], drecv.at[1, which, :, lanes]),
        lambda which, lanes: (dsend.at[0, which, :, lanes], drecv.at[0, which, :, lanes]),
        held_grad, edge_sems[5:],
    )
    pl.semaphore_wait(barrier, len(partners) + 2 * jnp.logical_or(x == 1, x == 2).astype(jnp.int32))

    def piece_at(block, at):
        return w.at[pl.ds(pl.multiple_of(block * BLOCK + at * PIECE, 16), PIECE)]

    def rest_at(block):
        return w.at[pl.ds(pl.multiple_of(block * BLOCK + 4 * PIECE, 16), REST)]

    def same(ref, device):
        return copies.start(ref, ref, device)

    w_z = []
    second = place(x, y, lax.rem(z + 2 + 4 * c, 8), c)
    for device in (along_z[0], along_z[6], second):
        mine = weight.at[pl.ds(pl.multiple_of(y * PIECE, 16), PIECE)]
        w_z.append(copies.start(mine, piece_at(dp, y), device))
        w_z.append(copies.start(weight.at[pl.ds(4 * PIECE, REST)], rest_at(dp), device))
    for group in (3, 4):
        keys_values.start_into(group)
    keys_values.start_over((0, 1, 2))
    keys_values.start_inner(ORDER)
    w_peer = [copies.start(weight, w.at[own], peer)]
    go_peer = copies.start(go.at[:, pl.ds(pl.multiple_of(1536 * (1 - c), 128), WIDE)], gop, peer)

    others = [lax.rem(zl + d, 4) * 2 + c for d in (1, 2, 3)]
    for copy in w_z:
        copy.wait_recv()
    w_free = [same(piece_at(block, y), free) for block in others]
    w_full = [same(piece_at(block, y), full) for block in others]
    for block in others:
        w_peer.append(same(piece_at(block, y), peer))
        w_peer.append(same(rest_at(block), peer))
    keys_values.pass_on()

    own_k.wait()
    own_v.wait()
    own_w.wait()

    def forward(h, carry):
        lanes = pl.ds(pl.multiple_of(h * HS, HS), HS)
        s = nt(q[:, lanes], kw[:, lanes]) * SCALE2 + bias[0:1, :]
        e = jnp.exp2(s - jnp.max(s, axis=-1, keepdims=True))
        p = (e * (1.0 / jnp.sum(e, axis=-1, keepdims=True))).astype(BF16)
        probs[h] = p
        mx[0, :, lanes] = nn(p, vw[:, lanes]).astype(BF16)
        return carry

    def w_arrived(sent, from_y):
        for block, copy in zip(others, sent):
            copy.wait_recv()
            w_peer.append(same(piece_at(block, from_y), peer))

    w_free[0].wait_recv()
    w_free[1].wait_recv()
    w_free[2].wait_recv()
    w_on = [same(piece_at(block, y_full), free) for block in others]
    for block in others:
        w_peer.append(same(piece_at(block, y_full), peer))
    for index, group in enumerate(ORDER):
        keys_values.wait(group)
        lax.fori_loop(*GROUPS[group], forward, 0)
    mx_peer = copies.start(mx.at[0], mx.at[1], peer)

    go_peer.wait_recv()
    mx_peer.wait_recv()

    def chunk(p, at):
        return term.at[p, pl.ds(pl.multiple_of(at * 416, 16), 416), pl.ds(0, WIDTH[p])]

    opposite = lax.rem(y + 2, 4)
    y_first, y_second, x_copies = [], [], []
    for p in (0, 1):
        first, size = HALF * p, WIDTH[p]

        def weight_term(step, carry):
            h = lax.rem((opposite * HEADS) // 4 + step, HEADS)
            lanes = pl.ds(pl.multiple_of(h * HS, HS), HS)
            columns = pl.ds(pl.multiple_of(1536 * c + first, 128), size)
            term[p, lanes, 0:size] = (
                tn(mx[0, :, lanes], go[:, columns]) + tn(mx[1, :, lanes], gop[:, first : first + size])
            ).astype(BF16)
            return carry

        lax.fori_loop(0, 4, weight_term, 0)
        y_first.append(copies.start(chunk(p, opposite), yr1.at[p, :, pl.ds(0, size)], free))
        lax.fori_loop(4, HEADS, weight_term, 0)
        y_second.append([copies.start(chunk(p, y_full), yr2.at[p, 1, :, pl.ds(0, size)], full)])

    def y_next(p):
        y_first[p].wait_recv()
        part = chunk(p, y_free)
        here = pl.ds(0, WIDTH[p])
        part[...] = (part[...].astype(F32) + yr1[p, :, here].astype(F32)).astype(BF16)
        y_second[p].append(copies.start(part, yr2.at[p, 0, :, here], free))

    w_arrived(w_full, y_free)
    w_arrived(w_on, lax.rem(y + 2, 4))
    for copy in w_peer:
        copy.wait_recv()

    def backward(h, carry):
        lanes = pl.ds(pl.multiple_of(h * HS, HS), HS)
        g = gm[:, lanes]
        p = probs[h]
        delta = jnp.sum(g.astype(F32) * mx[0, :, lanes].astype(F32), axis=-1, keepdims=True)
        ds = (p.astype(F32) * (nt(g, vw[:, lanes]) - delta)).astype(BF16)
        dq[:, lanes] = (nn(ds, kw[:, lanes]) * SCALE).astype(BF16)
        for which, grad in ((0, tn(ds, q[:, lanes]) * SCALE), (1, tn(p, g))):
            dsend[0, which, :, lanes] = grad[:ROWS].astype(BF16)
            down[which, :, lanes] = grad[ROWS : 2 * ROWS]
            dsend[1, which, :, lanes] = grad[2 * ROWS :].astype(BF16)
        return carry

    for index, group in enumerate(ORDER):
        first, last = GROUPS[group]
        lanes = pl.ds(first * HS, (last - first) * HS)
        gm[:, lanes] = nn(go[...], w[:, lanes]).astype(BF16)
        lax.fori_loop(first, last, backward, 0)
        if group > 2:
            grads.start_into(group)
        else:
            grads.start_over((group,))
        grads.start_inner((group,))
        if index == 4:
            y_next(0)

    for i in range(5):
        columns = pl.ds(i * 640, 640)
        res[:, columns] = nt(mx[0], w[columns, :]).astype(BF16)
    grads.pass_on()
    y_next(1)

    for p in (0, 1):
        for copy in y_second[p]:
            copy.wait_recv()
        here = pl.ds(0, WIDTH[p])
        ysum[pl.ds(0, 416), here] = (
            chunk(p, y)[...].astype(F32) + yr2[p, 0, :, here].astype(F32) + yr2[p, 1, :, here].astype(F32)
        )
        ysum[pl.ds(416, 16), :] = jnp.zeros((16, HALF), F32)
        for to in range(4):
            for half in range(2):
                xs[p, to, half, :, here] = ysum[pl.ds(208 * half + 52 * to, 64), here].astype(BF16)
        x_copies.append([
            copies.start(xs.at[p, lax.rem(x + d, 4), :, :, here], xr.at[p, d - 1, :, :, here], along_x[d - 1])
            for d in (1, 2, 3)
        ])

    def to_owner(p, half, b):
        at = p * 4 + half * 2 + b
        z_to = half * 4 + c * 2 + p
        slot = lax.rem(z + 8 - z_to, 8)
        mine = jnp.logical_and(z_to == z, c == b)
        return mine, at, pltpu.make_async_remote_copy(
            src_ref=zs.at[at], dst_ref=zr.at[slot], send_sem=z_send.at[at], recv_sem=z_recv.at[slot],
            device_id=place(x, y, z_to, b), device_id_type=MESH,
        )

    for p in (0, 1):
        for copy in x_copies[p]:
            copy.wait_recv()
        for half in range(2):
            here = pl.ds(0, WIDTH[p])
            total = xs[p, x, half, :, here].astype(F32)
            for i in range(3):
                total = total + xr[p, i, half, :, here].astype(F32)
            if p == 0:
                edge[half] = total[:, 768:]
            else:
                total = jnp.concatenate([edge[half], total], axis=1)
            for b in (0, 1):
                shift = lax.rem(2 * HALF - BLOCK * b - 32 * p - 64 * c, HALF)
                zs[p * 4 + half * 2 + b] = pltpu.roll(total, shift, 1)[:, :512].astype(BF16)
        for half in range(2):
            for b in (0, 1):
                mine, at, copy = to_owner(p, half, b)

                @pl.when(mine)
                def _():
                    zr[0] = zs[at]

                @pl.when(jnp.logical_not(mine))
                def _():
                    copy.start()

    def from_z(slot):
        return pltpu.make_async_remote_copy(
            src_ref=zs.at[0], dst_ref=zr.at[slot], send_sem=z_send.at[0], recv_sem=z_recv.at[slot],
            device_id=peer, device_id_type=MESH,
        )

    for slot in range(1, 8):
        from_z(slot).wait_recv()

    @pl.when(zl // 2 != c)
    def _():
        from_z(0).wait_recv()

    total = zr[0].astype(F32)
    for i in range(1, 8):
        total = total + zr[i].astype(F32)
    gw[...] = total[:52, :BLOCK].astype(BF16)

    for group in ORDER:
        first, last = GROUPS[group]
        lanes = pl.ds(first * HS, (last - first) * HS)
        grads.wait(group)
        for which, out in ((0, dk), (1, dv)):
            out[:, lanes] = (
                down[which, :, lanes]
                + drecv[0, which, :, lanes].astype(F32)
                + drecv[1, which, :, lanes].astype(F32)
            ).astype(BF16)
    for copy in copies.started:
        copy.wait_send()
    keys_values.drain()
    grads.drain()
    for p in (0, 1):
        for half in range(2):
            for b in (0, 1):
                mine, at, copy = to_owner(p, half, b)

                @pl.when(jnp.logical_not(mine))
                def _():
                    copy.wait_send()


PARTS = 4


def put_out(*refs):
    ins, outs, held = refs[:5], refs[5:10], refs[10:15]
    in_sem, out_sem = refs[15:]
    steps = []
    for i, (src, dst, via) in enumerate(zip(ins, outs, held)):
        parts = PARTS if i < 4 else 1
        rows = src.shape[0] // parts
        for j in range(parts):
            at = pl.ds(j * rows, rows)
            n = len(steps)
            a, b, c = (src, via, dst) if parts == 1 else (src.at[at], via.at[at], dst.at[at])
            steps.append((
                pltpu.make_async_copy(a, b, in_sem.at[n]),
                pltpu.make_async_copy(b, c, out_sem.at[n]),
            ))
    for first, _ in steps:
        first.start()
    for first, second in steps:
        first.wait()
        second.start()
    for _, second in steps:
        second.wait()


def on_device(queries, keys, values, grad_out, out_weight, frame_clip):
    vmem = pl.BlockSpec(memory_space=pltpu.VMEM)
    hbm = pl.BlockSpec(memory_space=pl.ANY)
    half = jax.ShapeDtypeStruct((ROWS, HD), BF16)
    edge = [pltpu.SemaphoreType.DMA((n,)) for n in (20, 20, 4, 4, 4)]
    res, dq, dk, dv, gw = pl.pallas_call(
        body,
        out_shape=(
            jax.ShapeDtypeStruct((ROWS, 8 * BLOCK), BF16),
            half,
            half,
            half,
            jax.ShapeDtypeStruct((52, BLOCK), BF16),
        ),
        in_specs=[vmem, hbm, hbm, vmem, hbm, pl.BlockSpec(memory_space=pltpu.SMEM)],
        out_specs=(vmem,) * 5,
        scratch_shapes=[
            pltpu.VMEM((3 * ROWS, HD), BF16),
            pltpu.VMEM((3 * ROWS, HD), BF16),
            pltpu.VMEM((8 * BLOCK, HD), BF16),
            pltpu.VMEM((8, 3 * ROWS), F32),
            pltpu.VMEM((HEADS, ROWS, 3 * ROWS), BF16),
            pltpu.VMEM((2, ROWS, HD), BF16),
            pltpu.VMEM((ROWS, HD), BF16),
            pltpu.VMEM((ROWS, WIDE), BF16),
            pltpu.VMEM((2, 2, ROWS, HD), BF16),
            pltpu.VMEM((2, 2, ROWS, HD), BF16),
            pltpu.VMEM((2, ROWS, HD), F32),
            pltpu.VMEM((2, 2, ROWS, 2 * HS), BF16),
            pltpu.VMEM((2, 2, ROWS, 2 * HS), BF16),
            pltpu.VMEM((2, HD, HALF), BF16),
            pltpu.VMEM((2, 416, HALF), BF16),
            pltpu.VMEM((2, 2, 416, HALF), BF16),
            pltpu.VMEM((432, HALF), F32),
            pltpu.VMEM((2, 64, HS), F32),
            pltpu.VMEM((2, 4, 2, 64, HALF), BF16),
            pltpu.VMEM((2, 3, 2, 64, HALF), BF16),
            pltpu.VMEM((8, 64, 512), BF16),
            pltpu.VMEM((8, 64, 512), BF16),
            pltpu.SemaphoreType.DMA((3,)),
            pltpu.SemaphoreType.DMA((N_COPIES,)),
            pltpu.SemaphoreType.DMA((N_COPIES,)),
            pltpu.SemaphoreType.DMA((8,)),
            pltpu.SemaphoreType.DMA((8,)),
        ] + edge + edge,
        compiler_params=pltpu.CompilerParams(
            collective_id=0, has_side_effects=True, vmem_limit_bytes=63 * 1024 * 1024
        ),
        cost_estimate=pl.CostEstimate(flops=12_100_000_000, bytes_accessed=25_000_000, transcendentals=2_600_000),
        name="attention_and_projection",
    )(queries[0], keys[0], values[0], grad_out[0], out_weight.T, frame_clip)
    outs = (res, dq, dk, dv, gw)
    res, dq, dk, dv, gw = pl.pallas_call(
        put_out,
        out_shape=tuple(jax.ShapeDtypeStruct(a.shape, a.dtype) for a in outs),
        in_specs=[hbm] * 5,
        out_specs=(hbm,) * 5,
        scratch_shapes=[pltpu.VMEM(a.shape, a.dtype) for a in outs]
        + [pltpu.SemaphoreType.DMA((4 * PARTS + 1,)), pltpu.SemaphoreType.DMA((4 * PARTS + 1,))],
        compiler_params=pltpu.CompilerParams(vmem_limit_bytes=60 * 1024 * 1024),
        name="outputs",
    )(*outs)
    return (res[None], dq[None], dk[None], dv[None], gw)


def solution(mesh):
    in_specs = (
        P("dp", "tm", None),
        P("dp", "tm", None),
        P("dp", "tm", None),
        P("dp", "tm", None),
        P(None, "dp"),
        P("dp", None),
    )
    out_specs = (
        P("dp", "tm", None),
        P("dp", "tm", None),
        P("dp", "tm", None),
        P("dp", "tm", None),
        P("tm", "dp"),
    )
    return jax.shard_map(
        on_device, mesh=mesh, in_specs=in_specs, out_specs=out_specs, check_vma=False
    )
```
